256 devices in a mesh: island: 8 (over x, core), dap: 32 (over z, y).
Axes of the slice: x: 4, y: 4, z: 8, core: 2. Of those that a mesh axis runs over, the one named last changes fastest.
Arguments:
- pair: bfloat16 [8, 384, 384, 128], P('island', 'dap'), may hold values from -6 to 6
- cotangent: bfloat16 [8, 384, 384, 128], P('island', 'dap'), may hold values from -6 to 6
- res_count: int32 [8], P('island'), may hold values from 192 to 384, as said below
- w_left: bfloat16 [128, 128], replicated, may hold values from -0.5 to 0.5
- w_left_gate: bfloat16 [128, 128], replicated, may hold values from -0.5 to 0.5
- w_right: bfloat16 [128, 128], replicated, may hold values from -0.5 to 0.5
- w_right_gate: bfloat16 [128, 128], replicated, may hold values from -0.5 to 0.5
- w_gate: bfloat16 [128, 128], replicated, may hold values from -0.5 to 0.5
- w_out: bfloat16 [128, 128], replicated, may hold values from -0.5 to 0.5
Outputs:
- grad_pair: bfloat16 [8, 384, 384, 128], P('island', 'dap')
- grad_left: float32 [128, 128], replicated
- grad_left_gate: float32 [128, 128], replicated
- grad_right: float32 [128, 128], replicated
- grad_right_gate: float32 [128, 128], replicated
- grad_gate: float32 [128, 128], replicated
- grad_out: float32 [128, 128], replicated
The draws below stay inside these ranges and needn't reach their ends.
Inputs may be any that keep to these rules, and one draw needn't show every extreme that they name: `res_count`: every count is at least 192, and some complex has all 384 residues.
All inputs are finite; a program needn't handle non-finite values.
Results may differ from the reference program's by a relative error of at most 0.0078.
Values may be sent and summed in bfloat16 or wider, within the bound.
No kernel may reach another device: no remote copies, remote signals or barrier semaphores. Data moves between devices by JAX's collectives and lax.ppermute only.
A program may use at most 128 MiB of HBM per device.

```python
import jax
import jax.numpy as jnp
from jax import lax

C = 128
R = 384
ISLANDS = 8


def draw_res_count(key, part):
    key = jax.random.fold_in(key, 7)
    first, second = jax.random.split(key)
    counts = jax.random.randint(first, (ISLANDS,), R // 2, R + 1)
    chosen = jax.random.randint(second, (), 0, ISLANDS)
    return jnp.where(jnp.arange(ISLANDS) == chosen, R, counts).astype(jnp.int32)


def levels(stream_key, shape, cuts, least, top_value):
    gain, own = 1.0, jax.random.fold_in(stream_key, 6)
    for position, shards_of in cuts:
        heights = jnp.exp(jax.random.uniform(jax.random.fold_in(own, position), (shards_of,), jnp.float32, least / len(cuts), top_value / len(cuts)))
        gain = gain * jnp.repeat(heights, shape[position] // shards_of).reshape([-1 if axis == position else 1 for axis in range(len(shape))])
    return gain


def centred(rng, shape, scale, most, cuts=(), held_as=jnp.bfloat16):
    result = scale * jax.random.normal(rng, shape, jnp.float32)
    if cuts:
        result = result * levels(rng, shape, cuts, -0.22, 0.18)
    return jnp.clip(result, -most, most).astype(held_as)


def setup_inputs(seed: int = 0) -> dict:
    key_list = jax.random.split(jax.random.key(seed), 10)
    pair = centred(key_list[0], (ISLANDS, R, R, C), 1.0, 6.0, ((0, 8), (1, 32)))
    cotangent = centred(key_list[1], (ISLANDS, R, R, C), 1.0, 6.0, ((0, 8), (1, 32)))
    res_count = draw_res_count(jax.random.fold_in(key_list[9], 71), 0)
    w_left = centred(key_list[3], (C, C), C ** -0.5, 0.5)
    w_left_gate = centred(key_list[4], (C, C), C ** -0.5, 0.5)
    w_right = centred(key_list[5], (C, C), C ** -0.5, 0.5)
    w_right_gate = centred(key_list[6], (C, C), C ** -0.5, 0.5)
    w_gate = centred(key_list[7], (C, C), C ** -0.5, 0.5)
    w_out = centred(key_list[8], (C, C), C ** -0.5, 0.5)
    return {"pair": pair, "cotangent": cotangent, "res_count": res_count, "w_left": w_left, "w_left_gate": w_left_gate, "w_right": w_right, "w_right_gate": w_right_gate, "w_gate": w_gate, "w_out": w_out}


def one_complex(pair_one, cot_one, count, w_left, w_left_gate, w_right, w_right_gate, w_gate, w_out):
    zf = pair_one.astype(jnp.float32)
    cells = jnp.arange(R)
    pair_residue_mask = ((cells[:, None] < count) & (cells[None, :] < count)).astype(jnp.float32)
    lproj = jnp.einsum('ikd,dc->cik', zf, w_left.astype(jnp.float32))
    lgate = jax.nn.sigmoid(jnp.einsum('ikd,dc->cik', zf, w_left_gate.astype(jnp.float32)))
    right_projected = jnp.einsum('ikd,dc->cik', zf, w_right.astype(jnp.float32))
    right_gate_value = jax.nn.sigmoid(jnp.einsum('ikd,dc->cik', zf, w_right_gate.astype(jnp.float32)))
    left = (pair_residue_mask * lgate * lproj).astype(jnp.bfloat16)
    right = (pair_residue_mask * right_gate_value * right_projected).astype(jnp.bfloat16)
    edges = jnp.einsum('cik,cjk->cij', left.astype(jnp.float32), right.astype(jnp.float32)).astype(jnp.bfloat16)
    edge_f = edges.astype(jnp.float32)
    mean_shifted = edge_f - lax.optimization_barrier(jnp.mean(edge_f, axis=0))
    inverse_deviation = lax.rsqrt(lax.optimization_barrier(jnp.mean(mean_shifted * mean_shifted, axis=0)) + 1e-05)
    standardized_input = mean_shifted * inverse_deviation
    layer_normed = (standardized_input * pair_residue_mask).astype(jnp.bfloat16)
    gate = jax.nn.sigmoid(jnp.einsum('ijd,do->ijo', zf, w_gate.astype(jnp.float32)))
    linear = jnp.einsum('cij,co->ijo', layer_normed.astype(jnp.float32), w_out.astype(jnp.float32))
    gcot = cot_one.astype(jnp.float32)
    dscaled = (gcot * gate).astype(jnp.bfloat16)
    dgate = (gcot * linear * gate * (1.0 - gate)).astype(jnp.bfloat16)
    normed_gradient = jnp.einsum('ijo,co->cij', dscaled.astype(jnp.float32), w_out.astype(jnp.float32))
    edge_gradient = (pair_residue_mask * inverse_deviation * (normed_gradient - lax.optimization_barrier(jnp.mean(normed_gradient, axis=0)) - standardized_input * lax.optimization_barrier(jnp.mean(normed_gradient * standardized_input, axis=0)))).astype(jnp.bfloat16)
    dleft = jnp.einsum('cij,cjk->cik', edge_gradient.astype(jnp.float32), right.astype(jnp.float32)).astype(jnp.bfloat16)
    right_gradient = jnp.einsum('cij,cik->cjk', edge_gradient.astype(jnp.float32), left.astype(jnp.float32)).astype(jnp.bfloat16)
    dlf = dleft.astype(jnp.float32) * pair_residue_mask
    right_full_gradient = right_gradient.astype(jnp.float32) * pair_residue_mask
    dlin_left = (dlf * lgate).astype(jnp.bfloat16).astype(jnp.float32)
    dgl = (dlf * lproj * lgate * (1.0 - lgate)).astype(jnp.bfloat16).astype(jnp.float32)
    right_linear_gradient = (right_full_gradient * right_gate_value).astype(jnp.bfloat16).astype(jnp.float32)
    right_gate_gradient = (right_full_gradient * right_projected * right_gate_value * (1.0 - right_gate_value)).astype(jnp.bfloat16).astype(jnp.float32)
    dgf = dgate.astype(jnp.float32)
    grad_pair = (jnp.einsum('ijo,do->ijd', dgf, w_gate.astype(jnp.float32)) + jnp.einsum('cij,dc->ijd', dlin_left, w_left.astype(jnp.float32)) + jnp.einsum('cij,dc->ijd', dgl, w_left_gate.astype(jnp.float32)) + jnp.einsum('cij,dc->ijd', right_linear_gradient, w_right.astype(jnp.float32)) + jnp.einsum('cij,dc->ijd', right_gate_gradient, w_right_gate.astype(jnp.float32))).astype(jnp.bfloat16)
    grad_left = jnp.einsum('ikd,cik->dc', zf, dlin_left)
    grad_left_gate = jnp.einsum('ikd,cik->dc', zf, dgl)
    grad_right = jnp.einsum('ikd,cik->dc', zf, right_linear_gradient)
    grad_right_gate = jnp.einsum('ikd,cik->dc', zf, right_gate_gradient)
    grad_gate = jnp.einsum('ijd,ijo->do', zf, dgf)
    grad_out = jnp.einsum('cij,ijo->co', layer_normed.astype(jnp.float32), dscaled.astype(jnp.float32))
    return (grad_pair, grad_left, grad_left_gate, grad_right, grad_right_gate, grad_gate, grad_out)

def reference(pair, cotangent, res_count, w_left, w_left_gate, w_right, w_right_gate, w_gate, w_out):

    def step(items):
        return one_complex(items[0], items[1], items[2], w_left, w_left_gate, w_right, w_right_gate, w_gate, w_out)
    outs = lax.map(step, (pair, cotangent, res_count))
    return (outs[0], lax.optimization_barrier(jnp.sum(outs[1], axis=0)), lax.optimization_barrier(jnp.sum(outs[2], axis=0)), lax.optimization_barrier(jnp.sum(outs[3], axis=0)), lax.optimization_barrier(jnp.sum(outs[4], axis=0)), lax.optimization_barrier(jnp.sum(outs[5], axis=0)), lax.optimization_barrier(jnp.sum(outs[6], axis=0)))
```

```python
import jax
import jax.numpy as jnp
from jax import lax
from jax.experimental import pallas as pl
from jax.experimental.pallas import tpu as pltpu
from jax.sharding import PartitionSpec as P

F32 = jnp.float32
BF16 = jnp.bfloat16
C = 128
HI = lax.Precision.HIGHEST


def dot(a, b, ca, cb, precision=None):
    return lax.dot_general(
        a, b, (((ca,), (cb,)), ((), ())), preferred_element_type=F32, precision=precision
    )


def iota(shape, dim):
    return lax.broadcasted_iota(jnp.int32, shape, dim)


def pick(side):
    row, chan = iota((2 * C, C), 0), iota((2 * C, C), 1)
    hit = ((row % 8) // 4 == side) & (chan == (row // 8) * 4 + row % 4)
    return hit.astype(F32)


def spread_rows(w_out):
    parts = [dot(pick(side).astype(BF16), w_out, 1, 0) for side in range(2)]
    return jnp.concatenate(parts, axis=1).astype(BF16)


def both_projections(w_left, w_left_gate, w_right, w_right_gate):
    on_left, on_right = pick(0).astype(BF16), pick(1).astype(BF16)
    proj = dot(on_left, w_left, 1, 1) + dot(on_right, w_right, 1, 1)
    gate = dot(on_left, w_left_gate, 1, 1) + dot(on_right, w_right_gate, 1, 1)
    return jnp.concatenate([proj, gate], axis=0).astype(BF16)


def row_mask(count, row, shape):
    return jnp.where((row < count) & (iota(shape, len(shape) - 1) < count), 1.0, 0.0)


def first_row(rows):
    return lax.axis_index("dap") * rows


def project_kernel(count_ref, z_ref, wl_ref, wlg_ref, wr_ref, wrg_ref, out_ref, w_ref):
    rows, total, _ = z_ref.shape
    count = count_ref[0]
    start = first_row(rows)
    w_ref[...] = both_projections(wl_ref[...], wlg_ref[...], wr_ref[...], wrg_ref[...])

    def body(m, carry):
        halves = []
        for h in range(2):
            i = 2 * m + h
            pg = dot(w_ref[...], z_ref[i], 1, 1)
            mask = row_mask(count, start + i, (1, total))
            made = mask * jax.nn.sigmoid(pg[2 * C :]) * pg[: 2 * C]
            halves.append(made.reshape(32, 8, total))
        at = pl.multiple_of(16 * m, 16)
        out_ref[:, pl.ds(at, 16), :] = jnp.concatenate(halves, axis=1).astype(BF16)
        return carry

    lax.fori_loop(0, rows // 2, body, 0)


def put_wide(ref, at, rows, value):
    for n in range(ref.shape[0]):
        ref[n, pl.ds(at, rows), :] = value[:, n * C : (n + 1) * C]


def take(ref, first, count, step):
    return jnp.concatenate(
        [ref[n, pl.ds(first, count, stride=step), :] for n in range(ref.shape[0])], axis=1
    )


def put(ref, first, count, step, value):
    for n in range(ref.shape[0]):
        ref[n, pl.ds(first, count, stride=step), :] = value[:, n * C : (n + 1) * C]


def get_rows(ref, at, rows):
    return jnp.concatenate([ref[n, pl.ds(at, rows), :] for n in range(ref.shape[0])], axis=1)


def edges_kernel(x_ref, out_ref, lr_ref, wide_ref, prod_ref):
    devices, block, total = x_ref.shape

    def widen(s, carry):
        put_wide(wide_ref, pl.multiple_of(s * block, block), block, x_ref[s].astype(F32))
        return carry

    lax.fori_loop(0, devices, widen, 0)
    for c in range(4):
        left = take(wide_ref, c, total, 8).astype(BF16)
        right = take(wide_ref, 4 + c, total, 8).astype(BF16)
        lr_ref[c] = left
        lr_ref[4 + c] = right
        put(prod_ref, c, total, 4, dot(left, right, 1, 1))

    def narrow(s, carry):
        at = pl.multiple_of(s * (block // 2), block // 2)
        out_ref[s] = get_rows(prod_ref, at, block // 2).astype(BF16)
        return carry

    lax.fori_loop(0, devices, narrow, 0)


def gates_kernel(z_ref, g_ref, wg_ref, wo_ref, ds_ref, fac_ref, dn_ref, wgt_ref, wx_ref):
    rows = z_ref.shape[0]
    wgt_ref[...] = wg_ref[...].astype(F32).T.astype(BF16)
    wx_ref[...] = spread_rows(wo_ref[...])

    def body(m, carry):
        for h in range(2):
            i = 2 * m + h
            gate = jax.nn.sigmoid(dot(wgt_ref[...], z_ref[i], 1, 1))
            scaled = g_ref[i].astype(F32).T * gate
            ds_ref[m, h * C : (h + 1) * C, :] = scaled.astype(BF16)
            fac_ref[m, h * C : (h + 1) * C, :] = scaled * (1.0 - gate)
        dn_ref[m] = dot(wx_ref[...], ds_ref[m], 1, 0)
        return carry

    lax.fori_loop(0, rows // 2, body, 0)


def chan_mean(x):
    s = jnp.sum(x, axis=0)
    top = iota(s.shape, 0) < 4
    first = jnp.sum(jnp.where(top, s, 0.0), axis=0, keepdims=True)
    second = jnp.sum(jnp.where(top, 0.0, s), axis=0, keepdims=True)
    return jnp.where(top, first, second) * (1.0 / C)


def norm_kernel(count_ref, e_ref, dn_ref, de_ref, nm_ref):
    devices, block, total = e_ref.shape
    rows = block // 4
    count = count_ref[0]
    start = first_row(rows)

    def body(q, carry):
        at = pl.multiple_of(16 * q, 16)
        e_all = e_ref[:, pl.ds(at, 16), :].astype(F32)
        halves = []
        for h in range(2):
            e = e_all[:, 8 * h : 8 * h + 8, :]
            row = start + 4 * q + 2 * h + iota((8, total), 0) // 4
            mask = row_mask(count, row, (8, total))
            shifted = e - chan_mean(e)[None]
            rs = lax.rsqrt(chan_mean(shifted * shifted) + 1e-05)
            xhat = shifted * rs[None]
            nm_ref[2 * q + h] = (xhat * mask[None]).reshape(2 * C, total).astype(BF16)
            dn = dn_ref[2 * q + h].reshape(32, 8, total)
            m1 = chan_mean(dn)
            m2 = chan_mean(dn * xhat)
            halves.append((mask * rs)[None] * (dn - m1[None] - xhat * m2[None]))
        de_ref[:, pl.ds(at, 16), :] = jnp.concatenate(halves, axis=1).astype(BF16)
        return carry

    lax.fori_loop(0, rows // 4, body, 0)


def linear_kernel(z_ref, nm_ref, ds_ref, fac_ref, wo_ref, dg_ref, gg_ref, go_ref, wx_ref, ga_ref, oa_ref):
    rows = z_ref.shape[0]
    wx_ref[...] = spread_rows(wo_ref[...]).astype(F32).T.astype(BF16)
    ga_ref[...] = jnp.zeros_like(ga_ref)
    oa_ref[...] = jnp.zeros_like(oa_ref)

    def body(m, carry):
        lin = dot(wx_ref[...], nm_ref[m], 1, 0)
        dg_ref[m] = (lin * fac_ref[m]).astype(BF16)
        for h in range(2):
            ga_ref[...] += dot(dg_ref[m, h * C : (h + 1) * C, :], z_ref[2 * m + h], 1, 0)
        oa_ref[...] += dot(nm_ref[m], ds_ref[m], 1, 1)
        return carry

    lax.fori_loop(0, rows // 2, body, 0)
    gg_ref[...] = ga_ref[...].T
    go_ref[...] = dot(pick(0), oa_ref[:, :C], 0, 0, HI) + dot(pick(1), oa_ref[:, C:], 0, 0, HI)


def back_kernel(x_ref, lr_ref, out_ref, wide_ref, prod_ref):
    devices, block, total = x_ref.shape

    def widen(s, carry):
        put_wide(wide_ref, pl.multiple_of(s * block, block), block, x_ref[s].astype(F32))
        return carry

    lax.fori_loop(0, devices, widen, 0)
    for c in range(4):
        de = take(wide_ref, c, total, 4)
        put(prod_ref, c, total, 8, dot(de.astype(BF16), lr_ref[4 + c], 1, 0))
        put(prod_ref, 4 + c, total, 8, dot(de.T.astype(BF16), lr_ref[c], 1, 0))

    def narrow(s, carry):
        at = pl.multiple_of(s * (2 * block), 2 * block)
        out_ref[s] = get_rows(prod_ref, at, 2 * block).astype(BF16)
        return carry

    lax.fori_loop(0, devices, narrow, 0)


def weights_kernel(
    count_ref, z_ref, d_ref, wl_ref, wlg_ref, wr_ref, wrg_ref, gg_ref, go_ref, x_ref, out_ref, w_ref, acc_ref
):
    rows, total, _ = z_ref.shape
    count = count_ref[0]
    start = first_row(rows)
    w_ref[...] = both_projections(wl_ref[...], wlg_ref[...], wr_ref[...], wrg_ref[...])
    acc_ref[...] = jnp.zeros_like(acc_ref)

    def body(m, carry):
        at = pl.multiple_of(16 * m, 16)
        both = d_ref[:, pl.ds(at, 16), :].astype(F32)
        for h in range(2):
            i = 2 * m + h
            d = both[:, 8 * h : 8 * h + 8, :].reshape(2 * C, total)
            d = d * row_mask(count, start + i, (1, total))
            pg = dot(w_ref[...], z_ref[i], 1, 1)
            gate = jax.nn.sigmoid(pg[2 * C :])
            dlin = d * gate
            x_ref[i, : 2 * C, :] = dlin.astype(BF16)
            x_ref[i, 2 * C :, :] = (dlin * pg[: 2 * C] * (1.0 - gate)).astype(BF16)
            acc_ref[...] += dot(x_ref[i], z_ref[i], 1, 0)
        return carry

    lax.fori_loop(0, rows // 2, body, 0)
    on_left, on_right = pick(0), pick(1)
    out_ref[0 * C : 1 * C, :] = dot(acc_ref[: 2 * C, :], on_left, 0, 0, HI)
    out_ref[1 * C : 2 * C, :] = dot(acc_ref[2 * C :, :], on_left, 0, 0, HI)
    out_ref[2 * C : 3 * C, :] = dot(acc_ref[: 2 * C, :], on_right, 0, 0, HI)
    out_ref[3 * C : 4 * C, :] = dot(acc_ref[2 * C :, :], on_right, 0, 0, HI)
    out_ref[4 * C : 5 * C, :] = gg_ref[...]
    out_ref[5 * C : 6 * C, :] = go_ref[...]


def pair_kernel(x_ref, dg_ref, wl_ref, wlg_ref, wr_ref, wrg_ref, wg_ref, out_ref, w_ref):
    rows = x_ref.shape[0]
    w_ref[...] = both_projections(wl_ref[...], wlg_ref[...], wr_ref[...], wrg_ref[...]).astype(F32).T.astype(BF16)

    def body(m, carry):
        for h in range(2):
            i = 2 * m + h
            made = dot(w_ref[...], x_ref[i], 1, 0) + dot(wg_ref[...], dg_ref[m, h * C : (h + 1) * C, :], 1, 0)
            out_ref[0, i] = made.T.astype(BF16)
        return carry

    lax.fori_loop(0, rows // 2, body, 0)


def call(body, outs, scratch, flops, *args, smem=()):
    specs = [
        pl.BlockSpec(memory_space=pltpu.SMEM if n in smem else pltpu.VMEM) for n in range(len(args))
    ]
    shapes = [jax.ShapeDtypeStruct(s, t) for s, t in outs]
    out_specs = [pl.BlockSpec(memory_space=pltpu.VMEM)] * len(outs)
    if len(outs) == 1:
        shapes, out_specs = shapes[0], out_specs[0]
    moved = sum(a.size * a.dtype.itemsize for a in args)
    return pl.pallas_call(
        body,
        out_shape=shapes,
        in_specs=specs,
        out_specs=out_specs,
        scratch_shapes=[pltpu.VMEM(s, t) for s, t in scratch],
        compiler_params=pltpu.CompilerParams(vmem_limit_bytes=40 << 20),
        cost_estimate=pl.CostEstimate(flops=flops, bytes_accessed=moved, transcendentals=0),
    )(*args)


def exchange(x, axis):
    return lax.all_to_all(x, axis, split_axis=0, concat_axis=0, tiled=True)


def on_device(
    pair, cotangent, res_count, w_left, w_left_gate, w_right, w_right_gate, w_gate, w_out
):
    z, g = pair[0], cotangent[0]
    rows, total, _ = z.shape
    pairs = rows // 2
    sides = (w_left, w_left_gate, w_right, w_right_gate)
    mega = 10**6

    blocks = call(
        project_kernel, [((32, 8 * rows, total), BF16)], [((4 * C, C), BF16)], 4000 * mega,
        res_count, z, *sides, smem=(0,),
    )
    blocks = exchange(blocks, "dap")
    scaled, factor, dnormed = call(
        gates_kernel,
        [((pairs, 2 * C, total), BF16), ((pairs, 2 * C, total), F32), ((pairs, 2 * C, total), F32)],
        [((C, C), BF16), ((2 * C, 2 * C), BF16)], 4000 * mega,
        z, g, w_gate, w_out,
    )
    edges, lr = call(
        edges_kernel,
        [((32, 4 * rows, total), BF16), ((8, total, total), BF16)],
        [((total // C, 8 * total, C), F32), ((total // C, 4 * total, C), F32)], 4000 * mega,
        blocks,
    )
    edges = exchange(edges, "dap")
    dedges, normed = call(
        norm_kernel,
        [((32, 4 * rows, total), BF16), ((pairs, 2 * C, total), BF16)], [], 4000 * mega,
        res_count, edges, dnormed, smem=(0,),
    )
    dedges = exchange(dedges, "dap")
    dgate, part_gate, part_out = call(
        linear_kernel,
        [((pairs, 2 * C, total), BF16), ((C, C), F32), ((C, C), F32)],
        [((2 * C, 2 * C), BF16), ((C, C), F32), ((2 * C, 2 * C), F32)], 4000 * mega,
        z, normed, scaled, factor, w_out,
    )
    back = call(
        back_kernel,
        [((32, 8 * rows, total), BF16)],
        [((total // C, 4 * total, C), F32), ((total // C, 8 * total, C), F32)], 4000 * mega,
        dedges, lr,
    )
    back = exchange(back, "dap")
    made, parts = call(
        weights_kernel,
        [((rows, 4 * C, total), BF16), ((6 * C, C), F32)],
        [((4 * C, C), BF16), ((4 * C, C), F32)], 4000 * mega,
        res_count, z, back, *sides, part_gate, part_out, smem=(0,),
    )
    share = exchange(parts.reshape(8, 96, C), "island").sum(axis=0)
    share = exchange(share.reshape(32, 3, C), "dap").sum(axis=0, keepdims=True)
    share = exchange(jnp.broadcast_to(share, (32, 3, C)), "dap").reshape(1, 96, C)
    whole = exchange(jnp.broadcast_to(share, (8, 96, C)), "island").reshape(6, C, C)
    grad = call(
        pair_kernel,
        [((1, rows, total, C), BF16)],
        [((C, 4 * C), BF16)], 4000 * mega,
        made, dgate, *sides, w_gate,
    )
    return (grad, *(whole[n] for n in range(6)))


def solution(mesh):
    rows = P("island", "dap", None, None)
    return jax.shard_map(
        on_device,
        mesh=mesh,
        in_specs=(rows, rows, P("island"), P(), P(), P(), P(), P(), P()),
        out_specs=(rows, P(), P(), P(), P(), P(), P()),
        check_vma=False,
    )
```

```python
import jax
import jax.numpy as jnp
from jax import lax
from jax.experimental import pallas as pl
from jax.experimental.pallas import tpu as pltpu
from jax.sharding import Mesh
from jax.sharding import PartitionSpec as P

F32 = jnp.float32
BF16 = jnp.bfloat16
C = 128
HI = lax.Precision.HIGHEST
ISLAND, DAP = ("x", "core"), ("z", "y")


def dot(a, b, ca, cb, precision=None):
    return lax.dot_general(
        a, b, (((ca,), (cb,)), ((), ())), preferred_element_type=F32, precision=precision
    )


def iota(shape, dim):
    return lax.broadcasted_iota(jnp.int32, shape, dim)


def pick(side):
    row, chan = iota((2 * C, C), 0), iota((2 * C, C), 1)
    hit = ((row % 8) // 4 == side) & (chan == (row // 8) * 4 + row % 4)
    return hit.astype(F32)


def spread_rows(w_out):
    parts = [dot(pick(side).astype(BF16), w_out, 1, 0) for side in range(2)]
    return jnp.concatenate(parts, axis=1).astype(BF16)


def both_projections(w_left, w_left_gate, w_right, w_right_gate):
    on_left, on_right = pick(0).astype(BF16), pick(1).astype(BF16)
    proj = dot(on_left, w_left, 1, 1) + dot(on_right, w_right, 1, 1)
    gate = dot(on_left, w_left_gate, 1, 1) + dot(on_right, w_right_gate, 1, 1)
    return jnp.concatenate([proj, gate], axis=0).astype(BF16)


def row_mask(count, row, shape):
    return jnp.where((row < count) & (iota(shape, len(shape) - 1) < count), 1.0, 0.0)


def first_row(rows):
    return lax.axis_index(DAP) * rows


def each(n, step):
    def body(m, carry):
        step(m)
        return carry

    lax.fori_loop(0, n, body, 0)


def two(m):
    return pl.ds(2 * m, 2)


def tile(m):
    return pl.ds(pl.multiple_of(16 * m, 16), 16)


def project_kernel(
    count_ref, z_hbm, wl_hbm, wlg_hbm, wr_hbm, wrg_hbm, out_hbm,
    w_ref, z_ref, side_ref, out_ref, z_sem, w_sem, out_sem,
):
    rows, total, _ = z_ref.shape
    count = count_ref[0]
    start = first_row(rows)
    sides = [
        pltpu.make_async_copy(ref, side_ref.at[n], w_sem.at[n])
        for n, ref in enumerate((wl_hbm, wlg_hbm, wr_hbm, wrg_hbm))
    ]
    for copy in sides:
        copy.start()

    def cells(m):
        return pltpu.make_async_copy(z_hbm.at[two(m)], z_ref.at[two(m)], z_sem.at[m])

    def sent(m):
        return pltpu.make_async_copy(out_ref.at[:, tile(m)], out_hbm.at[:, tile(m)], out_sem.at[m])

    each(rows // 2, lambda m: cells(m).start())
    for copy in sides:
        copy.wait()
    w_ref[...] = both_projections(side_ref[0], side_ref[1], side_ref[2], side_ref[3])

    def step(m):
        cells(m).wait()
        halves = []
        for h in range(2):
            i = 2 * m + h
            pg = dot(w_ref[...], z_ref[i], 1, 1)
            mask = row_mask(count, start + i, (1, total))
            made = mask * jax.nn.sigmoid(pg[2 * C :]) * pg[: 2 * C]
            halves.append(made.reshape(32, 8, total))
        out_ref[:, tile(m), :] = jnp.concatenate(halves, axis=1).astype(BF16)
        sent(m).start()

    each(rows // 2, step)
    each(rows // 2, lambda m: sent(m).wait())


def factors_kernel(count_ref, z_ref, wl_ref, wlg_ref, wr_ref, wrg_ref, out_ref, w_ref):
    rows, total, _ = z_ref.shape
    count = count_ref[0]
    start = first_row(rows)
    w_ref[...] = both_projections(wl_ref[...], wlg_ref[...], wr_ref[...], wrg_ref[...])

    def body(i, carry):
        pg = dot(w_ref[...], z_ref[i], 1, 1)
        gate = jax.nn.sigmoid(pg[2 * C :])
        masked = gate * row_mask(count, start + i, (1, total))
        out_ref[i, : 2 * C, :] = masked.astype(BF16)
        out_ref[i, 2 * C :, :] = (masked * pg[: 2 * C] * (1.0 - gate)).astype(BF16)
        return carry

    lax.fori_loop(0, rows, body, 0)


def put_wide(ref, at, rows, value):
    for n in range(ref.shape[0]):
        ref[n, pl.ds(at, rows), :] = value[:, n * C : (n + 1) * C]


def take(ref, first, count, step):
    return jnp.concatenate(
        [ref[n, pl.ds(first, count, stride=step), :] for n in range(ref.shape[0])], axis=1
    )


def put(ref, first, count, step, value):
    for n in range(ref.shape[0]):
        ref[n, pl.ds(first, count, stride=step), :] = value[:, n * C : (n + 1) * C]


def get_rows(ref, at, rows):
    return jnp.concatenate([ref[n, pl.ds(at, rows), :] for n in range(ref.shape[0])], axis=1)


def widen_all(x_hbm, x_ref, wide_ref, sem):
    devices, block, _ = x_ref.shape
    part = devices // 4

    def copy(n):
        here = pl.ds(n * part, part)
        return pltpu.make_async_copy(x_hbm.at[here], x_ref.at[here], sem.at[n])

    def widen(s):
        put_wide(wide_ref, pl.multiple_of(s * block, block), block, x_ref[s].astype(F32))

    def step(n):
        copy(n).wait()
        each(part, lambda s: widen(n * part + s))

    return lambda: each(4, lambda n: copy(n).start()), lambda: each(4, step)


def edges_kernel(x_hbm, out_hbm, lr_hbm, wide_ref, prod_ref, lr_ref, x_ref, out_ref, lr_sem, x_sem, out_sem):
    total = x_ref.shape[2]
    fetch, widen = widen_all(x_hbm, x_ref, wide_ref, x_sem)
    fetch()
    widen()

    def kept(c):
        return pltpu.make_async_copy(lr_ref.at[two(c)], lr_hbm.at[two(c)], lr_sem.at[c])

    for c in range(4):
        left = take(wide_ref, c, total, 8).astype(BF16)
        right = take(wide_ref, 4 + c, total, 8).astype(BF16)
        lr_ref[2 * c] = left
        lr_ref[2 * c + 1] = right
        kept(c).start()
        put(prod_ref, c, total, 4, dot(left, right, 1, 1))
    for copy in narrowed(prod_ref, out_ref, out_hbm, out_sem):
        copy.wait()
    each(4, lambda c: kept(c).wait())


def narrowed(prod_ref, out_ref, out_hbm, sem):
    devices, block, _ = out_ref.shape
    part = devices // 4
    copies = []
    for n in range(4):

        def narrow(s, carry):
            at = pl.multiple_of(s * block, block)
            out_ref[s] = get_rows(prod_ref, at, block).astype(BF16)
            return carry

        lax.fori_loop(n * part, (n + 1) * part, narrow, 0)
        here = pl.ds(n * part, part)
        copies.append(pltpu.make_async_copy(out_ref.at[here], out_hbm.at[here], sem.at[n]))
        copies[-1].start()
    return copies


def gates_kernel(z_ref, g_ref, wg_ref, wo_ref, ds_ref, fac_ref, dn_ref, wgt_ref, wx_ref):
    rows = z_ref.shape[0]
    wgt_ref[...] = wg_ref[...].astype(F32).T.astype(BF16)
    wx_ref[...] = spread_rows(wo_ref[...])

    def body(m, carry):
        for h in range(2):
            i = 2 * m + h
            gate = jax.nn.sigmoid(dot(wgt_ref[...], z_ref[i], 1, 1))
            scaled = g_ref[i].astype(F32).T * gate
            ds_ref[m, h * C : (h + 1) * C, :] = scaled.astype(BF16)
            fac_ref[m, h * C : (h + 1) * C, :] = scaled * (1.0 - gate)
        dn_ref[m] = dot(wx_ref[...], ds_ref[m], 1, 0)
        return carry

    lax.fori_loop(0, rows // 2, body, 0)


def chan_mean(x):
    s = jnp.sum(x, axis=0)
    top = iota(s.shape, 0) < 4
    first = jnp.sum(jnp.where(top, s, 0.0), axis=0, keepdims=True)
    second = jnp.sum(jnp.where(top, 0.0, s), axis=0, keepdims=True)
    return jnp.where(top, first, second) * (1.0 / C)


def norm_kernel(
    count_ref, e_hbm, dn_hbm, de_hbm, nm_hbm, e_ref, dn_ref, de_ref, nm_ref, e_sem, dn_sem, de_sem, nm_sem
):
    devices, block, total = e_ref.shape
    rows = block // 4
    count = count_ref[0]
    start = first_row(rows)

    def came(q):
        return (
            pltpu.make_async_copy(e_hbm.at[:, tile(q)], e_ref.at[:, tile(q)], e_sem.at[q]),
            pltpu.make_async_copy(dn_hbm.at[two(q)], dn_ref.at[two(q)], dn_sem.at[q]),
        )

    def gone(q):
        return (
            pltpu.make_async_copy(de_ref.at[:, tile(q)], de_hbm.at[:, tile(q)], de_sem.at[q]),
            pltpu.make_async_copy(nm_ref.at[two(q)], nm_hbm.at[two(q)], nm_sem.at[q]),
        )

    def begin(q):
        for copy in came(q):
            copy.start()

    def finish(q):
        for copy in gone(q):
            copy.wait()

    def step(q):
        for copy in came(q):
            copy.wait()
        e_all = e_ref[:, tile(q), :].astype(F32)
        halves = []
        for h in range(2):
            e = e_all[:, 8 * h : 8 * h + 8, :]
            row = start + 4 * q + 2 * h + iota((8, total), 0) // 4
            mask = row_mask(count, row, (8, total))
            shifted = e - chan_mean(e)[None]
            rs = lax.rsqrt(chan_mean(shifted * shifted) + 1e-05)
            xhat = shifted * rs[None]
            nm_ref[2 * q + h] = (xhat * mask[None]).reshape(2 * C, total).astype(BF16)
            dn = dn_ref[2 * q + h].reshape(32, 8, total)
            m1 = chan_mean(dn)
            m2 = chan_mean(dn * xhat)
            halves.append((mask * rs)[None] * (dn - m1[None] - xhat * m2[None]))
        de_ref[:, tile(q), :] = jnp.concatenate(halves, axis=1).astype(BF16)
        for copy in gone(q):
            copy.start()

    each(rows // 4, begin)
    each(rows // 4, step)
    each(rows // 4, finish)


def linear_kernel(z_ref, nm_ref, ds_ref, fac_ref, wo_ref, dg_ref, sums_ref, wx_ref, ga_ref, oa_ref):
    rows = z_ref.shape[0]
    wx_ref[...] = spread_rows(wo_ref[...]).astype(F32).T.astype(BF16)
    ga_ref[...] = jnp.zeros_like(ga_ref)
    oa_ref[...] = jnp.zeros_like(oa_ref)

    def body(m, carry):
        lin = dot(wx_ref[...], nm_ref[m], 1, 0)
        dg_ref[m] = (lin * fac_ref[m]).astype(BF16)
        for h in range(2):
            ga_ref[...] += dot(dg_ref[m, h * C : (h + 1) * C, :], z_ref[2 * m + h], 1, 0)
        oa_ref[...] += dot(nm_ref[m], ds_ref[m], 1, 1)
        return carry

    lax.fori_loop(0, rows // 2, body, 0)
    sums_ref[:C, :] = ga_ref[...].T
    sums_ref[C:, :] = dot(pick(0), oa_ref[:, :C], 0, 0, HI) + dot(pick(1), oa_ref[:, C:], 0, 0, HI)


def back_kernel(x_hbm, lr_hbm, out_hbm, wide_ref, prod_ref, lr_ref, x_ref, out_ref, lr_sem, x_sem, out_sem):
    total = x_ref.shape[2]

    def kept(c):
        return pltpu.make_async_copy(lr_hbm.at[two(c)], lr_ref.at[two(c)], lr_sem.at[c])

    fetch, widen = widen_all(x_hbm, x_ref, wide_ref, x_sem)
    fetch()
    each(4, lambda c: kept(c).start())
    widen()
    for c in range(4):
        de = take(wide_ref, c, total, 4)
        kept(c).wait()
        put(prod_ref, c, total, 8, dot(de.astype(BF16), lr_ref[2 * c + 1], 1, 0))
        put(prod_ref, 4 + c, total, 8, dot(de.T.astype(BF16), lr_ref[2 * c], 1, 0))
    for copy in narrowed(prod_ref, out_ref, out_hbm, out_sem):
        copy.wait()


def by_side(x):
    x = x.reshape(16, 2, 8, C)
    even, odd = x[:, 0], x[:, 1]
    top = iota((16, 8, C), 1) < 4
    left = jnp.where(top, even, pltpu.roll(odd, 4, 1))
    right = jnp.where(top, pltpu.roll(even, 4, 1), odd)
    return left.reshape(C, C), right.reshape(C, C)


def side_gradients(d_ref, fac_ref, m, h):
    d = d_ref[:, tile(m), :].astype(F32)[:, 8 * h : 8 * h + 8, :].reshape(2 * C, -1)
    factor = fac_ref[2 * m + h].astype(F32)
    return jnp.concatenate([d * factor[: 2 * C], d * factor[2 * C :]], axis=0).astype(BF16)


def weights_kernel(
    z_hbm, d_hbm, fac_hbm, sums_hbm, out_ref, acc_ref, z_ref, d_ref, fac_ref, z_sem, d_sem, fac_sem, sums_sem
):
    rows, total, _ = z_ref.shape

    def came(m):
        return (
            pltpu.make_async_copy(d_hbm.at[:, tile(m)], d_ref.at[:, tile(m)], d_sem.at[m]),
            pltpu.make_async_copy(fac_hbm.at[two(m)], fac_ref.at[two(m)], fac_sem.at[m]),
            pltpu.make_async_copy(z_hbm.at[two(m)], z_ref.at[two(m)], z_sem.at[m]),
        )

    def begin(m):
        for copy in came(m):
            copy.start()

    def step(m):
        for copy in came(m):
            copy.wait()
        for h in range(2):
            acc_ref[...] += dot(side_gradients(d_ref, fac_ref, m, h), z_ref[2 * m + h], 1, 0)

    each(rows // 2, begin)
    rest = pltpu.make_async_copy(sums_hbm, out_ref.at[pl.ds(4 * C, 2 * C)], sums_sem.at[0])
    rest.start()
    acc_ref[...] = jnp.zeros_like(acc_ref)
    each(rows // 2, step)
    for n in range(2):
        left, right = by_side(acc_ref[2 * C * n : 2 * C * (n + 1), :])
        out_ref[n * C : (n + 1) * C, :] = left.T
        out_ref[(2 + n) * C : (3 + n) * C, :] = right.T
    rest.wait()


def pair_kernel(d_ref, fac_ref, dg_ref, w_ref, wg_ref, out_ref, wt_ref):
    rows = fac_ref.shape[0]
    wt_ref[...] = w_ref[...].astype(F32).T.astype(BF16)

    def body(m, carry):
        for h in range(2):
            i = 2 * m + h
            made = dot(wt_ref[...], side_gradients(d_ref, fac_ref, m, h), 1, 0)
            made += dot(wg_ref[...], dg_ref[m, h * C : (h + 1) * C, :], 1, 0)
            out_ref[0, i] = made.T.astype(BF16)
        return carry

    lax.fori_loop(0, rows // 2, body, 0)


def call(body, outs, scratch, flops, *args, smem=(), hbm=(), hbm_out=(), sems=()):
    spaces = [pltpu.SMEM if n in smem else pltpu.HBM if n in hbm else pltpu.VMEM for n in range(len(args))]
    shapes = [jax.ShapeDtypeStruct(s, t) for s, t in outs]
    out_specs = [
        pl.BlockSpec(memory_space=pltpu.HBM if n in hbm_out else pltpu.VMEM) for n in range(len(outs))
    ]
    if len(outs) == 1:
        shapes, out_specs = shapes[0], out_specs[0]
    moved = sum(a.size * a.dtype.itemsize for a in args)
    return pl.pallas_call(
        body,
        out_shape=shapes,
        in_specs=[pl.BlockSpec(memory_space=space) for space in spaces],
        out_specs=out_specs,
        scratch_shapes=[pltpu.VMEM(s, t) for s, t in scratch] + [pltpu.SemaphoreType.DMA((n,)) for n in sems],
        compiler_params=pltpu.CompilerParams(vmem_limit_bytes=62 << 20),
        cost_estimate=pl.CostEstimate(flops=flops, bytes_accessed=moved, transcendentals=0),
    )(*args)


def exchange(x, axis):
    return lax.all_to_all(x, axis, split_axis=0, concat_axis=0, tiled=True)


def on_device(
    pair, cotangent, res_count, w_left, w_left_gate, w_right, w_right_gate, w_gate, w_out
):
    z, g = pair[0], cotangent[0]
    rows, total, _ = z.shape
    pairs = rows // 2
    sides = (w_left, w_left_gate, w_right, w_right_gate)
    mega = 10**6

    blocks = call(
        project_kernel, [((32, 8 * rows, total), BF16)],
        [((4 * C, C), BF16), ((rows, total, C), BF16), ((4, C, C), BF16), ((32, 8 * rows, total), BF16)],
        4000 * mega, res_count, z, *sides, smem=(0,), hbm=(1, 2, 3, 4, 5), hbm_out=(0,), sems=(pairs, 4, pairs),
    )
    blocks = exchange(blocks, DAP)
    factors, w_all = call(
        factors_kernel, [((rows, 4 * C, total), BF16), ((4 * C, C), BF16)], [], 4000 * mega,
        res_count, z, *sides, smem=(0,),
    )
    scaled, factor, dnormed = call(
        gates_kernel,
        [((pairs, 2 * C, total), BF16), ((pairs, 2 * C, total), F32), ((pairs, 2 * C, total), F32)],
        [((C, C), BF16), ((2 * C, 2 * C), BF16)], 4000 * mega,
        z, g, w_gate, w_out,
    )
    edges, lr = call(
        edges_kernel,
        [((32, 4 * rows, total), BF16), ((8, total, total), BF16)],
        [
            ((total // C, 8 * total, C), F32), ((total // C, 4 * total, C), F32),
            ((8, total, total), BF16), ((32, 8 * rows, total), BF16), ((32, 4 * rows, total), BF16),
        ], 4000 * mega,
        blocks, hbm=(0,), hbm_out=(0, 1), sems=(4, 4, 4),
    )
    edges = exchange(edges, DAP)
    dedges, normed = call(
        norm_kernel,
        [((32, 4 * rows, total), BF16), ((pairs, 2 * C, total), BF16)],
        [
            ((32, 4 * rows, total), BF16), ((pairs, 2 * C, total), F32),
            ((32, 4 * rows, total), BF16), ((pairs, 2 * C, total), BF16),
        ], 4000 * mega,
        res_count, edges, dnormed, smem=(0,), hbm=(1, 2), hbm_out=(0, 1), sems=(rows // 4,) * 4,
    )
    dedges = exchange(dedges, DAP)
    dgate, sums = call(
        linear_kernel,
        [((pairs, 2 * C, total), BF16), ((2 * C, C), F32)],
        [((2 * C, 2 * C), BF16), ((C, C), F32), ((2 * C, 2 * C), F32)], 4000 * mega,
        z, normed, scaled, factor, w_out,
    )
    back = call(
        back_kernel,
        [((32, 8 * rows, total), BF16)],
        [
            ((total // C, 4 * total, C), F32), ((total // C, 8 * total, C), F32),
            ((8, total, total), BF16), ((32, 4 * rows, total), BF16), ((32, 8 * rows, total), BF16),
        ], 4000 * mega,
        dedges, lr, hbm=(0, 1), hbm_out=(0,), sems=(4, 4, 4),
    )
    back = exchange(back, DAP)
    parts = call(
        weights_kernel,
        [((6 * C, C), F32)],
        [
            ((4 * C, C), F32), ((rows, total, C), BF16),
            ((32, 8 * rows, total), BF16), ((rows, 4 * C, total), BF16),
        ], 4000 * mega,
        z, back, factors, sums, hbm=(0, 1, 2, 3), sems=(pairs, pairs, pairs, 1),
    )
    near = ("x", "core", "y")
    share = exchange(parts.reshape(32, 24, C), near).sum(axis=0, keepdims=True)
    share = exchange(jnp.broadcast_to(share, (8, 24, C)), "z").sum(axis=0, keepdims=True)
    whole = exchange(jnp.broadcast_to(share, (32, 24, C)), near).reshape(6, C, C)
    grad = call(
        pair_kernel,
        [((1, rows, total, C), BF16)],
        [((C, 4 * C), BF16)], 4000 * mega,
        back, factors, dgate, w_all, w_gate,
    )
    return (grad, *(whole[n] for n in range(6)))


def solution(mesh):
    chips = Mesh(mesh.devices.reshape(4, 2, 8, 4), ISLAND + DAP)
    rows = P(ISLAND, DAP, None, None)
    return jax.shard_map(
        on_device,
        mesh=chips,
        in_specs=(rows, rows, P(ISLAND), P(), P(), P(), P(), P(), P()),
        out_specs=(rows, P(), P(), P(), P(), P(), P()),
        check_vma=False,
    )
```

```python
import jax
import jax.numpy as jnp
from jax import lax
from jax.experimental import pallas as pl
from jax.experimental.pallas import tpu as pltpu
from jax.sharding import Mesh
from jax.sharding import PartitionSpec as P

F32 = jnp.float32
BF16 = jnp.bfloat16
C = 128
HI = lax.Precision.HIGHEST
ISLAND, DAP = ("x", "core"), ("z", "y")


def dot(a, b, ca, cb, precision=None):
    return lax.dot_general(
        a, b, (((ca,), (cb,)), ((), ())), preferred_element_type=F32, precision=precision
    )


def iota(shape, dim):
    return lax.broadcasted_iota(jnp.int32, shape, dim)


def pick(side):
    row, chan = iota((2 * C, C), 0), iota((2 * C, C), 1)
    hit = ((row % 8) // 4 == side) & (chan == (row // 8) * 4 + row % 4)
    return hit.astype(F32)


def spread_rows(w_out):
    parts = [dot(pick(side).astype(BF16), w_out, 1, 0) for side in range(2)]
    return jnp.concatenate(parts, axis=1).astype(BF16)


def both_projections(w_left, w_left_gate, w_right, w_right_gate):
    on_left, on_right = pick(0).astype(BF16), pick(1).astype(BF16)
    proj = dot(on_left, w_left, 1, 1) + dot(on_right, w_right, 1, 1)
    gate = dot(on_left, w_left_gate, 1, 1) + dot(on_right, w_right_gate, 1, 1)
    return jnp.concatenate([proj, gate], axis=0).astype(BF16)


def row_mask(count, row, shape):
    return jnp.where((row < count) & (iota(shape, len(shape) - 1) < count), 1.0, 0.0)


def first_row(rows):
    return lax.axis_index(DAP) * rows


def each(n, step):
    def body(m, carry):
        step(m)
        return carry

    lax.fori_loop(0, n, body, 0)


def two(m):
    return pl.ds(2 * m, 2)


def tile(m):
    return pl.ds(pl.multiple_of(16 * m, 16), 16)


def project_kernel(
    count_ref, z_hbm, wl_hbm, wlg_hbm, wr_hbm, wrg_hbm, out_hbm,
    w_ref, z_ref, side_ref, out_ref, z_sem, w_sem, out_sem,
):
    rows, total, _ = z_ref.shape
    count = count_ref[0]
    start = first_row(rows)
    sides = [
        pltpu.make_async_copy(ref, side_ref.at[n], w_sem.at[n])
        for n, ref in enumerate((wl_hbm, wlg_hbm, wr_hbm, wrg_hbm))
    ]
    for copy in sides:
        copy.start()

    def cells(m):
        return pltpu.make_async_copy(z_hbm.at[two(m)], z_ref.at[two(m)], z_sem.at[m])

    def sent(m):
        return pltpu.make_async_copy(out_ref.at[:, tile(m)], out_hbm.at[:, tile(m)], out_sem.at[m])

    each(rows // 2, lambda m: cells(m).start())
    for copy in sides:
        copy.wait()
    w_ref[...] = both_projections(side_ref[0], side_ref[1], side_ref[2], side_ref[3])

    def step(m):
        cells(m).wait()
        halves = []
        for h in range(2):
            i = 2 * m + h
            pg = dot(w_ref[...], z_ref[i], 1, 1)
            mask = row_mask(count, start + i, (1, total))
            made = mask * jax.nn.sigmoid(pg[2 * C :]) * pg[: 2 * C]
            halves.append(made.reshape(32, 8, total))
        out_ref[:, tile(m), :] = jnp.concatenate(halves, axis=1).astype(BF16)
        sent(m).start()

    each(rows // 2, step)
    each(rows // 2, lambda m: sent(m).wait())


def factors_kernel(count_ref, z_ref, wl_ref, wlg_ref, wr_ref, wrg_ref, out_ref, w_ref):
    rows, total, _ = z_ref.shape
    count = count_ref[0]
    start = first_row(rows)
    w_ref[...] = both_projections(wl_ref[...], wlg_ref[...], wr_ref[...], wrg_ref[...])

    def body(i, carry):
        pg = dot(w_ref[...], z_ref[i], 1, 1)
        gate = jax.nn.sigmoid(pg[2 * C :])
        masked = gate * row_mask(count, start + i, (1, total))
        out_ref[i, : 2 * C, :] = masked.astype(BF16)
        out_ref[i, 2 * C :, :] = (masked * pg[: 2 * C] * (1.0 - gate)).astype(BF16)
        return carry

    lax.fori_loop(0, rows, body, 0)


def put_wide(ref, at, rows, value):
    for n in range(ref.shape[0]):
        ref[n, pl.ds(at, rows), :] = value[:, n * C : (n + 1) * C]


def take(ref, first, count, step):
    return jnp.concatenate(
        [ref[n, pl.ds(first, count, stride=step), :] for n in range(ref.shape[0])], axis=1
    )


def put(ref, first, count, step, value):
    for n in range(ref.shape[0]):
        ref[n, pl.ds(first, count, stride=step), :] = value[:, n * C : (n + 1) * C]


def get_rows(ref, at, rows):
    return jnp.concatenate([ref[n, pl.ds(at, rows), :] for n in range(ref.shape[0])], axis=1)


def widen_all(x_hbm, x_ref, wide_ref, sem):
    devices, block, _ = x_ref.shape
    part = devices // 4

    def copy(n):
        here = pl.ds(n * part, part)
        return pltpu.make_async_copy(x_hbm.at[here], x_ref.at[here], sem.at[n])

    def widen(s):
        put_wide(wide_ref, pl.multiple_of(s * block, block), block, x_ref[s].astype(F32))

    def step(n):
        copy(n).wait()
        each(part, lambda s: widen(n * part + s))

    return lambda: each(4, lambda n: copy(n).start()), lambda: each(4, step)


def edges_kernel(x_hbm, out_hbm, lr_hbm, wide_ref, prod_ref, lr_ref, x_ref, out_ref, lr_sem, x_sem, out_sem):
    total = x_ref.shape[2]
    fetch, widen = widen_all(x_hbm, x_ref, wide_ref, x_sem)
    fetch()
    widen()

    def kept(c):
        return pltpu.make_async_copy(lr_ref.at[two(c)], lr_hbm.at[two(c)], lr_sem.at[c])

    for c in range(4):
        left = take(wide_ref, c, total, 8).astype(BF16)
        right = take(wide_ref, 4 + c, total, 8).astype(BF16)
        lr_ref[2 * c] = left
        lr_ref[2 * c + 1] = right
        kept(c).start()
        put(prod_ref, c, total, 4, dot(left, right, 1, 1))
    for copy in narrowed(prod_ref, out_ref, out_hbm, out_sem):
        copy.wait()
    each(4, lambda c: kept(c).wait())


def narrowed(prod_ref, out_ref, out_hbm, sem):
    devices, block, _ = out_ref.shape
    part = devices // 4
    copies = []
    for n in range(4):

        def narrow(s, carry):
            at = pl.multiple_of(s * block, block)
            out_ref[s] = get_rows(prod_ref, at, block).astype(BF16)
            return carry

        lax.fori_loop(n * part, (n + 1) * part, narrow, 0)
        here = pl.ds(n * part, part)
        copies.append(pltpu.make_async_copy(out_ref.at[here], out_hbm.at[here], sem.at[n]))
        copies[-1].start()
    return copies


def gates_kernel(z_ref, g_ref, wg_ref, wo_ref, ds_ref, fac_ref, dn_ref, wgt_ref, wx_ref):
    rows = z_ref.shape[0]
    wgt_ref[...] = wg_ref[...].astype(F32).T.astype(BF16)
    wx_ref[...] = spread_rows(wo_ref[...])

    def body(m, carry):
        for h in range(2):
            i = 2 * m + h
            gate = jax.nn.sigmoid(dot(wgt_ref[...], z_ref[i], 1, 1))
            scaled = g_ref[i].astype(F32).T * gate
            ds_ref[m, h * C : (h + 1) * C, :] = scaled.astype(BF16)
            fac_ref[m, h * C : (h + 1) * C, :] = scaled * (1.0 - gate)
        dn_ref[m] = dot(wx_ref[...], ds_ref[m], 1, 0)
        return carry

    lax.fori_loop(0, rows // 2, body, 0)


def chan_mean(x):
    s = jnp.sum(x, axis=0)
    top = iota(s.shape, 0) < 4
    first = jnp.sum(jnp.where(top, s, 0.0), axis=0, keepdims=True)
    second = jnp.sum(jnp.where(top, 0.0, s), axis=0, keepdims=True)
    return jnp.where(top, first, second) * (1.0 / C)


def norm_kernel(
    count_ref, e_hbm, dn_hbm, de_hbm, nm_hbm, e_ref, dn_ref, de_ref, nm_ref, e_sem, dn_sem, de_sem, nm_sem
):
    devices, block, total = e_ref.shape
    rows = block // 4
    count = count_ref[0]
    start = first_row(rows)

    def came(q):
        return (
            pltpu.make_async_copy(e_hbm.at[:, tile(q)], e_ref.at[:, tile(q)], e_sem.at[q]),
            pltpu.make_async_copy(dn_hbm.at[two(q)], dn_ref.at[two(q)], dn_sem.at[q]),
        )

    def gone(q):
        return (
            pltpu.make_async_copy(de_ref.at[:, tile(q)], de_hbm.at[:, tile(q)], de_sem.at[q]),
            pltpu.make_async_copy(nm_ref.at[two(q)], nm_hbm.at[two(q)], nm_sem.at[q]),
        )

    def begin(q):
        for copy in came(q):
            copy.start()

    def finish(q):
        for copy in gone(q):
            copy.wait()

    def step(q):
        for copy in came(q):
            copy.wait()
        e_all = e_ref[:, tile(q), :].astype(F32)
        halves = []
        for h in range(2):
            e = e_all[:, 8 * h : 8 * h + 8, :]
            row = start + 4 * q + 2 * h + iota((8, total), 0) // 4
            mask = row_mask(count, row, (8, total))
            shifted = e - chan_mean(e)[None]
            rs = lax.rsqrt(chan_mean(shifted * shifted) + 1e-05)
            xhat = shifted * rs[None]
            nm_ref[2 * q + h] = (xhat * mask[None]).reshape(2 * C, total).astype(BF16)
            dn = dn_ref[2 * q + h].reshape(32, 8, total)
            m1 = chan_mean(dn)
            m2 = chan_mean(dn * xhat)
            halves.append((mask * rs)[None] * (dn - m1[None] - xhat * m2[None]))
        de_ref[:, tile(q), :] = jnp.concatenate(halves, axis=1).astype(BF16)
        for copy in gone(q):
            copy.start()

    each(rows // 4, begin)
    each(rows // 4, step)
    each(rows // 4, finish)


def linear_kernel(z_ref, nm_ref, ds_ref, fac_ref, wo_ref, dg_ref, sums_ref, wx_ref, ga_ref, oa_ref):
    rows = z_ref.shape[0]
    wx_ref[...] = spread_rows(wo_ref[...]).astype(F32).T.astype(BF16)
    ga_ref[...] = jnp.zeros_like(ga_ref)
    oa_ref[...] = jnp.zeros_like(oa_ref)

    def body(m, carry):
        lin = dot(wx_ref[...], nm_ref[m], 1, 0)
        dg_ref[m] = (lin * fac_ref[m]).astype(BF16)
        for h in range(2):
            ga_ref[...] += dot(dg_ref[m, h * C : (h + 1) * C, :], z_ref[2 * m + h], 1, 0)
        oa_ref[...] += dot(nm_ref[m], ds_ref[m], 1, 1)
        return carry

    lax.fori_loop(0, rows // 2, body, 0)
    sums_ref[:C, :] = ga_ref[...].T
    sums_ref[C:, :] = dot(pick(0), oa_ref[:, :C], 0, 0, HI) + dot(pick(1), oa_ref[:, C:], 0, 0, HI)


def back_kernel(x_hbm, lr_hbm, out_hbm, wide_ref, prod_ref, lr_ref, x_ref, out_ref, lr_sem, x_sem, out_sem):
    total = x_ref.shape[2]

    def kept(c):
        return pltpu.make_async_copy(lr_hbm.at[two(c)], lr_ref.at[two(c)], lr_sem.at[c])

    fetch, widen = widen_all(x_hbm, x_ref, wide_ref, x_sem)
    fetch()
    each(4, lambda c: kept(c).start())
    widen()
    for c in range(4):
        de = take(wide_ref, c, total, 4).astype(BF16)
        kept(c).wait()
        put(prod_ref, c, total, 8, dot(de, lr_ref[2 * c + 1], 1, 0))
        put(prod_ref, 4 + c, total, 8, dot(de, lr_ref[2 * c], 0, 0))
    for copy in narrowed(prod_ref, out_ref, out_hbm, out_sem):
        copy.wait()


def by_side(x):
    x = x.reshape(16, 2, 8, C)
    even, odd = x[:, 0], x[:, 1]
    top = iota((16, 8, C), 1) < 4
    left = jnp.where(top, even, pltpu.roll(odd, 4, 1))
    right = jnp.where(top, pltpu.roll(even, 4, 1), odd)
    return left.reshape(C, C), right.reshape(C, C)


def side_gradients(d_ref, fac_ref, m, h):
    d = d_ref[:, tile(m), :].astype(F32)[:, 8 * h : 8 * h + 8, :].reshape(2 * C, -1)
    factor = fac_ref[2 * m + h].astype(F32)
    return jnp.concatenate([d * factor[: 2 * C], d * factor[2 * C :]], axis=0).astype(BF16)


def weights_kernel(
    z_hbm, d_hbm, fac_hbm, sums_hbm, keep_ref, give_ref, out_ref, acc_ref, z_ref, d_ref, fac_ref,
    z_sem, d_sem, fac_sem, sums_sem,
):
    rows, total, _ = z_ref.shape

    def came(m):
        return (
            pltpu.make_async_copy(d_hbm.at[:, tile(m)], d_ref.at[:, tile(m)], d_sem.at[m]),
            pltpu.make_async_copy(fac_hbm.at[two(m)], fac_ref.at[two(m)], fac_sem.at[m]),
            pltpu.make_async_copy(z_hbm.at[two(m)], z_ref.at[two(m)], z_sem.at[m]),
        )

    def begin(m):
        for copy in came(m):
            copy.start()

    def step(m):
        for copy in came(m):
            copy.wait()
        made = jnp.concatenate([side_gradients(d_ref, fac_ref, m, h) for h in range(2)], axis=1)
        acc_ref[...] += dot(made, z_ref[two(m)].reshape(2 * total, C), 1, 0)

    each(rows // 2, begin)
    rest = pltpu.make_async_copy(sums_hbm, out_ref.at[pl.ds(4 * C, 2 * C)], sums_sem.at[0])
    rest.start()
    acc_ref[...] = jnp.zeros_like(acc_ref)
    each(rows // 2, step)
    for n in range(2):
        left, right = by_side(acc_ref[2 * C * n : 2 * C * (n + 1), :])
        out_ref[n * C : (n + 1) * C, :] = left.T
        out_ref[(2 + n) * C : (3 + n) * C, :] = right.T
    rest.wait()
    half = 3 * C
    keep = pl.multiple_of(lax.axis_index("core") * half, half)
    keep_ref[...] = out_ref[pl.ds(keep, half), :]
    give_ref[...] = out_ref[pl.ds(half - keep, half), :]


def pair_kernel(d_ref, fac_ref, dg_ref, w_ref, wg_ref, out_ref, wt_ref):
    rows = fac_ref.shape[0]
    wt_ref[...] = w_ref[...].astype(F32).T.astype(BF16)

    def body(m, carry):
        for h in range(2):
            i = 2 * m + h
            made = dot(wt_ref[...], side_gradients(d_ref, fac_ref, m, h), 1, 0)
            made += dot(wg_ref[...], dg_ref[m, h * C : (h + 1) * C, :], 1, 0)
            out_ref[0, i] = made.T.astype(BF16)
        return carry

    lax.fori_loop(0, rows // 2, body, 0)


def call(body, outs, scratch, flops, *args, smem=(), hbm=(), hbm_out=(), sems=(), after=(), limit=62):
    given = len(args)
    args = (*args, *after)
    hbm = (*hbm, *range(given, len(args)))

    def inner(*refs):
        body(*refs[:given], *refs[given + len(after) :])

    spaces = [pltpu.SMEM if n in smem else pltpu.HBM if n in hbm else pltpu.VMEM for n in range(len(args))]
    shapes = [jax.ShapeDtypeStruct(s, t) for s, t in outs]
    out_specs = [
        pl.BlockSpec(memory_space=pltpu.HBM if n in hbm_out else pltpu.VMEM) for n in range(len(outs))
    ]
    if len(outs) == 1:
        shapes, out_specs = shapes[0], out_specs[0]
    moved = sum(a.size * a.dtype.itemsize for a in args)
    return pl.pallas_call(
        inner,
        out_shape=shapes,
        in_specs=[pl.BlockSpec(memory_space=space) for space in spaces],
        out_specs=out_specs,
        scratch_shapes=[pltpu.VMEM(s, t) for s, t in scratch] + [pltpu.SemaphoreType.DMA((n,)) for n in sems],
        compiler_params=pltpu.CompilerParams(vmem_limit_bytes=limit << 20),
        cost_estimate=pl.CostEstimate(flops=flops, bytes_accessed=moved, transcendentals=0),
    )(*args)


def exchange(x, axis):
    return lax.all_to_all(x, axis, split_axis=0, concat_axis=0, tiled=True)


def swap(x):
    return lax.ppermute(x, "core", [(0, 1), (1, 0)])


def on_device(
    pair, cotangent, res_count, w_left, w_left_gate, w_right, w_right_gate, w_gate, w_out
):
    z, g = pair[0], cotangent[0]
    rows, total, _ = z.shape
    pairs = rows // 2
    sides = (w_left, w_left_gate, w_right, w_right_gate)
    mega = 10**6

    blocks = call(
        project_kernel, [((32, 8 * rows, total), BF16)],
        [((4 * C, C), BF16), ((rows, total, C), BF16), ((4, C, C), BF16), ((32, 8 * rows, total), BF16)],
        4000 * mega, res_count, z, *sides, smem=(0,), hbm=(1, 2, 3, 4, 5), hbm_out=(0,), sems=(pairs, 4, pairs),
    )
    factors, w_all = call(
        factors_kernel, [((rows, 4 * C, total), BF16), ((4 * C, C), BF16)], [], 4000 * mega,
        res_count, z, *sides, smem=(0,), after=(blocks,),
    )
    scaled, factor, dnormed = call(
        gates_kernel,
        [((pairs, 2 * C, total), BF16), ((pairs, 2 * C, total), F32), ((pairs, 2 * C, total), F32)],
        [((C, C), BF16), ((2 * C, 2 * C), BF16)], 4000 * mega,
        z, g, w_gate, w_out, after=(blocks,),
    )
    blocks = exchange(blocks, DAP)
    edges, lr = call(
        edges_kernel,
        [((32, 4 * rows, total), BF16), ((8, total, total), BF16)],
        [
            ((total // C, 8 * total, C), F32), ((total // C, 4 * total, C), F32),
            ((8, total, total), BF16), ((32, 8 * rows, total), BF16), ((32, 4 * rows, total), BF16),
        ], 4000 * mega,
        blocks, hbm=(0,), hbm_out=(0, 1), sems=(4, 4, 4), after=(factors, dnormed),
    )
    edges = exchange(edges, DAP)
    dedges, normed = call(
        norm_kernel,
        [((32, 4 * rows, total), BF16), ((pairs, 2 * C, total), BF16)],
        [
            ((32, 4 * rows, total), BF16), ((pairs, 2 * C, total), F32),
            ((32, 4 * rows, total), BF16), ((pairs, 2 * C, total), BF16),
        ], 4000 * mega,
        res_count, edges, dnormed, smem=(0,), hbm=(1, 2), hbm_out=(0, 1), sems=(rows // 4,) * 4,
    )
    dedges = exchange(dedges, DAP)
    back = call(
        back_kernel,
        [((32, 8 * rows, total), BF16)],
        [
            ((total // C, 4 * total, C), F32), ((total // C, 8 * total, C), F32),
            ((8, total, total), BF16), ((32, 4 * rows, total), BF16), ((32, 8 * rows, total), BF16),
        ], 4000 * mega,
        dedges, lr, hbm=(0, 1), hbm_out=(0,), sems=(4, 4, 4),
    )
    dgate, sums = call(
        linear_kernel,
        [((pairs, 2 * C, total), BF16), ((2 * C, C), F32)],
        [((2 * C, 2 * C), BF16), ((C, C), F32), ((2 * C, 2 * C), F32)], 4000 * mega,
        z, normed, scaled, factor, w_out, after=(back,),
    )
    back = exchange(back, DAP)
    keep, give = call(
        weights_kernel,
        [((3 * C, C), F32), ((3 * C, C), F32)],
        [
            ((6 * C, C), F32), ((4 * C, C), F32), ((rows, total, C), BF16),
            ((32, 8 * rows, total), BF16), ((rows, 4 * C, total), BF16),
        ], 4000 * mega,
        z, back, factors, sums, hbm=(0, 1, 2, 3), sems=(pairs, pairs, pairs, 1),
    )
    share = exchange((keep + swap(give)).reshape(16, 24, C), ("x", "y")).sum(axis=0, keepdims=True)
    share = exchange(jnp.broadcast_to(share, (8, 24, C)), "z").sum(axis=0, keepdims=True)
    share = jnp.broadcast_to(share, (16, 24, C))
    grad = call(
        pair_kernel,
        [((1, rows, total, C), BF16)],
        [((C, 4 * C), BF16)], 4000 * mega,
        back, factors, dgate, w_all, w_gate, after=(share,),
    )
    mine, grad = lax.optimization_barrier((exchange(share, ("x", "y")), grad))
    mine = mine.reshape(3, C, C)
    other = swap(mine)
    first = lax.axis_index("core") == 0
    whole = [jnp.where(first, mine[n], other[n]) for n in range(3)]
    whole += [jnp.where(first, other[n], mine[n]) for n in range(3)]
    return (grad, *whole)


def solution(mesh):
    chips = Mesh(mesh.devices.reshape(4, 2, 8, 4), ISLAND + DAP)
    rows = P(ISLAND, DAP, None, None)
    return jax.shard_map(
        on_device,
        mesh=chips,
        in_specs=(rows, rows, P(ISLAND), P(), P(), P(), P(), P(), P()),
        out_specs=(rows, P(), P(), P(), P(), P(), P()),
        check_vma=False,
    )
```

```python
import jax
import jax.numpy as jnp
from jax import lax
from jax.experimental import pallas as pl
from jax.experimental.pallas import tpu as pltpu
from jax.sharding import Mesh
from jax.sharding import PartitionSpec as P

F32 = jnp.float32
BF16 = jnp.bfloat16
C = 128
HI = lax.Precision.HIGHEST
ISLAND, DAP = ("x", "core"), ("z", "y")


def dot(a, b, ca, cb, precision=None):
    return lax.dot_general(
        a, b, (((ca,), (cb,)), ((), ())), preferred_element_type=F32, precision=precision
    )


def iota(shape, dim):
    return lax.broadcasted_iota(jnp.int32, shape, dim)


def pick(side):
    row, chan = iota((2 * C, C), 0), iota((2 * C, C), 1)
    hit = ((row % 8) // 4 == side) & (chan == (row // 8) * 4 + row % 4)
    return hit.astype(F32)


def spread_rows(w_out):
    parts = [dot(pick(side).astype(BF16), w_out, 1, 0) for side in range(2)]
    return jnp.concatenate(parts, axis=1).astype(BF16)


def both_projections(w_left, w_left_gate, w_right, w_right_gate):
    on_left, on_right = pick(0).astype(BF16), pick(1).astype(BF16)
    proj = dot(on_left, w_left, 1, 1) + dot(on_right, w_right, 1, 1)
    gate = dot(on_left, w_left_gate, 1, 1) + dot(on_right, w_right_gate, 1, 1)
    return jnp.concatenate([proj, gate], axis=0).astype(BF16)


def row_mask(count, row, shape):
    return jnp.where((row < count) & (iota(shape, len(shape) - 1) < count), 1.0, 0.0)


def first_row(rows):
    return lax.axis_index(DAP) * rows


def each(n, step):
    def body(m, carry):
        step(m)
        return carry

    lax.fori_loop(0, n, body, 0)


def two(m):
    return pl.ds(2 * m, 2)


def tile(m):
    return pl.ds(pl.multiple_of(16 * m, 16), 16)


def project_kernel(
    count_ref, z_hbm, wl_hbm, wlg_hbm, wr_hbm, wrg_hbm, out_hbm,
    w_ref, z_ref, side_ref, out_ref, z_sem, w_sem, out_sem,
):
    rows, total, _ = z_ref.shape
    count = count_ref[0]
    start = first_row(rows)
    sides = [
        pltpu.make_async_copy(ref, side_ref.at[n], w_sem.at[n])
        for n, ref in enumerate((wl_hbm, wlg_hbm, wr_hbm, wrg_hbm))
    ]
    for copy in sides:
        copy.start()

    def cells(m):
        return pltpu.make_async_copy(z_hbm.at[two(m)], z_ref.at[two(m)], z_sem.at[m])

    def sent(m):
        return pltpu.make_async_copy(out_ref.at[:, tile(m)], out_hbm.at[:, tile(m)], out_sem.at[m])

    each(rows // 2, lambda m: cells(m).start())
    for copy in sides:
        copy.wait()
    w_ref[...] = both_projections(side_ref[0], side_ref[1], side_ref[2], side_ref[3])

    def step(m):
        cells(m).wait()
        halves = []
        for h in range(2):
            i = 2 * m + h
            pg = dot(w_ref[...], z_ref[i], 1, 1)
            mask = row_mask(count, start + i, (1, total))
            made = mask * jax.nn.sigmoid(pg[2 * C :]) * pg[: 2 * C]
            halves.append(made.reshape(32, 8, total))
        out_ref[:, tile(m), :] = jnp.concatenate(halves, axis=1).astype(BF16)
        sent(m).start()

    each(rows // 2, step)
    each(rows // 2, lambda m: sent(m).wait())


def factors_kernel(count_ref, z_ref, wl_ref, wlg_ref, wr_ref, wrg_ref, out_ref, w_ref):
    rows, total, _ = z_ref.shape
    count = count_ref[0]
    start = first_row(rows)
    w_ref[...] = both_projections(wl_ref[...], wlg_ref[...], wr_ref[...], wrg_ref[...])

    def body(i, carry):
        pg = dot(w_ref[...], z_ref[i], 1, 1)
        gate = jax.nn.sigmoid(pg[2 * C :])
        masked = gate * row_mask(count, start + i, (1, total))
        out_ref[i, : 2 * C, :] = masked.astype(BF16)
        out_ref[i, 2 * C :, :] = (masked * pg[: 2 * C] * (1.0 - gate)).astype(BF16)
        return carry

    lax.fori_loop(0, rows, body, 0)


def put_wide(ref, at, rows, value):
    for n in range(ref.shape[0]):
        ref[n, pl.ds(at, rows), :] = value[:, n * C : (n + 1) * C]


def take(ref, first, count, step):
    return jnp.concatenate(
        [ref[n, pl.ds(first, count, stride=step), :] for n in range(ref.shape[0])], axis=1
    )


def put(ref, first, count, step, value):
    for n in range(ref.shape[0]):
        ref[n, pl.ds(first, count, stride=step), :] = value[:, n * C : (n + 1) * C]


def get_rows(ref, at, rows):
    return jnp.concatenate([ref[n, pl.ds(at, rows), :] for n in range(ref.shape[0])], axis=1)


def widen_all(x_hbm, x_ref, wide_ref, sem):
    devices, block, _ = x_ref.shape
    part = devices // 4

    def copy(n):
        here = pl.ds(n * part, part)
        return pltpu.make_async_copy(x_hbm.at[here], x_ref.at[here], sem.at[n])

    def widen(s):
        put_wide(wide_ref, pl.multiple_of(s * block, block), block, x_ref[s].astype(F32))

    def step(n):
        copy(n).wait()
        each(part, lambda s: widen(n * part + s))

    return lambda: each(4, lambda n: copy(n).start()), lambda: each(4, step)


def edges_kernel(x_hbm, out_hbm, wide_ref, prod_ref, x_ref, out_ref, x_sem, out_sem):
    total = x_ref.shape[2]
    fetch, widen = widen_all(x_hbm, x_ref, wide_ref, x_sem)
    fetch()
    widen()
    for c in range(4):
        left = take(wide_ref, c, total, 8).astype(BF16)
        right = take(wide_ref, 4 + c, total, 8).astype(BF16)
        put(prod_ref, c, total, 4, dot(left, right, 1, 1))
    for copy in narrowed(prod_ref, out_ref, out_hbm, out_sem):
        copy.wait()


def split_kernel(x_hbm, out_ref, wide_ref, x_ref, x_sem):
    total = x_ref.shape[2]
    fetch, widen = widen_all(x_hbm, x_ref, wide_ref, x_sem)
    fetch()
    widen()
    for c in range(4):
        out_ref[2 * c] = take(wide_ref, c, total, 8).astype(BF16)
        out_ref[2 * c + 1] = take(wide_ref, 4 + c, total, 8).astype(BF16)


def narrowed(prod_ref, out_ref, out_hbm, sem):
    devices, block, _ = out_ref.shape
    part = devices // 4
    copies = []
    for n in range(4):

        def narrow(s, carry):
            at = pl.multiple_of(s * block, block)
            out_ref[s] = get_rows(prod_ref, at, block).astype(BF16)
            return carry

        lax.fori_loop(n * part, (n + 1) * part, narrow, 0)
        here = pl.ds(n * part, part)
        copies.append(pltpu.make_async_copy(out_ref.at[here], out_hbm.at[here], sem.at[n]))
        copies[-1].start()
    return copies


def gates_kernel(z_ref, g_ref, wg_ref, wo_ref, ds_ref, fac_ref, wx_ref, dn_ref, wgt_ref):
    rows = z_ref.shape[0]
    wgt_ref[...] = wg_ref[...].astype(F32).T.astype(BF16)
    wx_ref[...] = spread_rows(wo_ref[...])

    def body(m, carry):
        for h in range(2):
            i = 2 * m + h
            gate = jax.nn.sigmoid(dot(wgt_ref[...], z_ref[i], 1, 1))
            scaled = g_ref[i].astype(F32).T * gate
            ds_ref[m, h * C : (h + 1) * C, :] = scaled.astype(BF16)
            fac_ref[m, h * C : (h + 1) * C, :] = scaled * (1.0 - gate)
        dn_ref[m] = dot(wx_ref[...], ds_ref[m], 1, 0)
        return carry

    lax.fori_loop(0, rows // 2, body, 0)


def chan_mean(x):
    s = jnp.sum(x, axis=0)
    top = iota(s.shape, 0) < 4
    first = jnp.sum(jnp.where(top, s, 0.0), axis=0, keepdims=True)
    second = jnp.sum(jnp.where(top, 0.0, s), axis=0, keepdims=True)
    return jnp.where(top, first, second) * (1.0 / C)


def standard(e):
    shifted = e - chan_mean(e)[None]
    rs = lax.rsqrt(chan_mean(shifted * shifted) + 1e-05)
    return shifted * rs[None], rs


def cell_mask(count, row, total):
    return row_mask(count, row + iota((8, total), 0) // 4, (8, total))


def norm_kernel(count_ref, e_hbm, dn_hbm, de_hbm, e_ref, dn_ref, de_ref, e_sem, dn_sem, de_sem):
    devices, block, total = e_ref.shape
    rows = block // 4
    count = count_ref[0]
    start = first_row(rows)

    def came(q):
        return (
            pltpu.make_async_copy(e_hbm.at[:, tile(q)], e_ref.at[:, tile(q)], e_sem.at[q]),
            pltpu.make_async_copy(dn_hbm.at[two(q)], dn_ref.at[two(q)], dn_sem.at[q]),
        )

    def gone(q):
        return pltpu.make_async_copy(de_ref.at[:, tile(q)], de_hbm.at[:, tile(q)], de_sem.at[q])

    def begin(q):
        for copy in came(q):
            copy.start()

    def step(q):
        for copy in came(q):
            copy.wait()
        e_all = e_ref[:, tile(q), :].astype(F32)
        halves = []
        for h in range(2):
            xhat, rs = standard(e_all[:, 8 * h : 8 * h + 8, :])
            mask = cell_mask(count, start + 4 * q + 2 * h, total)
            dn = dn_ref[2 * q + h].reshape(32, 8, total)
            m1 = chan_mean(dn)
            m2 = chan_mean(dn * xhat)
            halves.append((mask * rs)[None] * (dn - m1[None] - xhat * m2[None]))
        de_ref[:, tile(q), :] = jnp.concatenate(halves, axis=1).astype(BF16)
        gone(q).start()

    each(rows // 4, begin)
    each(rows // 4, step)
    each(rows // 4, lambda q: gone(q).wait())


def linear_kernel(count_ref, z_ref, e_ref, ds_ref, fac_ref, wx_in_ref, dg_ref, sums_ref, wx_ref, nm_ref, ga_ref, oa_ref):
    rows, total, _ = z_ref.shape
    count = count_ref[0]
    start = first_row(rows)

    def normalize(q):
        e_all = e_ref[:, tile(q), :].astype(F32)
        for h in range(2):
            xhat, _ = standard(e_all[:, 8 * h : 8 * h + 8, :])
            mask = cell_mask(count, start + 4 * q + 2 * h, total)
            nm_ref[2 * q + h] = (xhat * mask[None]).reshape(2 * C, total).astype(BF16)

    each(rows // 4, normalize)
    wx_ref[...] = wx_in_ref[...].astype(F32).T.astype(BF16)
    ga_ref[...] = jnp.zeros_like(ga_ref)
    oa_ref[...] = jnp.zeros_like(oa_ref)

    def body(m, carry):
        lin = dot(wx_ref[...], nm_ref[m], 1, 0)
        dg_ref[m] = (lin * fac_ref[m]).astype(BF16)
        for h in range(2):
            ga_ref[...] += dot(dg_ref[m, h * C : (h + 1) * C, :], z_ref[2 * m + h], 1, 0)
        oa_ref[...] += dot(nm_ref[m], ds_ref[m], 1, 1)
        return carry

    lax.fori_loop(0, rows // 2, body, 0)
    sums_ref[:C, :] = ga_ref[...].T
    sums_ref[C:, :] = dot(pick(0), oa_ref[:, :C], 0, 0, HI) + dot(pick(1), oa_ref[:, C:], 0, 0, HI)


def back_kernel(x_hbm, lr_hbm, out_hbm, wide_ref, prod_ref, lr_ref, x_ref, out_ref, lr_sem, x_sem, out_sem):
    total = x_ref.shape[2]

    def kept(c):
        return pltpu.make_async_copy(lr_hbm.at[two(c)], lr_ref.at[two(c)], lr_sem.at[c])

    fetch, widen = widen_all(x_hbm, x_ref, wide_ref, x_sem)
    fetch()
    each(4, lambda c: kept(c).start())
    widen()
    for c in range(4):
        de = take(wide_ref, c, total, 4).astype(BF16)
        kept(c).wait()
        put(prod_ref, c, total, 8, dot(de, lr_ref[2 * c + 1], 1, 0))
        put(prod_ref, 4 + c, total, 8, dot(de, lr_ref[2 * c], 0, 0))
    for copy in narrowed(prod_ref, out_ref, out_hbm, out_sem):
        copy.wait()


def by_side(x):
    x = x.reshape(16, 2, 8, C)
    even, odd = x[:, 0], x[:, 1]
    top = iota((16, 8, C), 1) < 4
    left = jnp.where(top, even, pltpu.roll(odd, 4, 1))
    right = jnp.where(top, pltpu.roll(even, 4, 1), odd)
    return left.reshape(C, C), right.reshape(C, C)


def side_gradients(d_ref, fac_ref, m, h):
    d = d_ref[:, tile(m), :].astype(F32)[:, 8 * h : 8 * h + 8, :].reshape(2 * C, -1)
    factor = fac_ref[2 * m + h].astype(F32)
    return jnp.concatenate([d * factor[: 2 * C], d * factor[2 * C :]], axis=0).astype(BF16)


def weights_kernel(
    z_hbm, d_hbm, fac_hbm, sums_hbm, keep_ref, give_ref, out_ref, acc_ref, z_ref, d_ref, fac_ref,
    z_sem, d_sem, fac_sem, sums_sem,
):
    rows, total, _ = z_ref.shape

    def came(m):
        return (
            pltpu.make_async_copy(d_hbm.at[:, tile(m)], d_ref.at[:, tile(m)], d_sem.at[m]),
            pltpu.make_async_copy(fac_hbm.at[two(m)], fac_ref.at[two(m)], fac_sem.at[m]),
            pltpu.make_async_copy(z_hbm.at[two(m)], z_ref.at[two(m)], z_sem.at[m]),
        )

    def begin(m):
        for copy in came(m):
            copy.start()

    def step(m):
        for copy in came(m):
            copy.wait()
        made = jnp.concatenate([side_gradients(d_ref, fac_ref, m, h) for h in range(2)], axis=1)
        acc_ref[...] += dot(made, z_ref[two(m)].reshape(2 * total, C), 1, 0)

    each(rows // 2, begin)
    rest = pltpu.make_async_copy(sums_hbm, out_ref.at[pl.ds(4 * C, 2 * C)], sums_sem.at[0])
    rest.start()
    acc_ref[...] = jnp.zeros_like(acc_ref)
    each(rows // 2, step)
    for n in range(2):
        left, right = by_side(acc_ref[2 * C * n : 2 * C * (n + 1), :])
        out_ref[n * C : (n + 1) * C, :] = left.T
        out_ref[(2 + n) * C : (3 + n) * C, :] = right.T
    rest.wait()
    half = 3 * C
    keep = pl.multiple_of(lax.axis_index("core") * half, half)
    keep_ref[...] = out_ref[pl.ds(keep, half), :]
    give_ref[...] = out_ref[pl.ds(half - keep, half), :]


def pair_kernel(d_ref, fac_ref, dg_ref, w_ref, wg_ref, out_ref, wt_ref):
    rows = fac_ref.shape[0]
    wt_ref[...] = w_ref[...].astype(F32).T.astype(BF16)

    def body(m, carry):
        for h in range(2):
            i = 2 * m + h
            made = dot(wt_ref[...], side_gradients(d_ref, fac_ref, m, h), 1, 0)
            made += dot(wg_ref[...], dg_ref[m, h * C : (h + 1) * C, :], 1, 0)
            out_ref[0, i] = made.T.astype(BF16)
        return carry

    lax.fori_loop(0, rows // 2, body, 0)


def call(body, outs, scratch, flops, *args, smem=(), hbm=(), hbm_out=(), sems=(), after=(), limit=62):
    given = len(args)
    args = (*args, *after)
    hbm = (*hbm, *range(given, len(args)))

    def inner(*refs):
        body(*refs[:given], *refs[given + len(after) :])

    spaces = [pltpu.SMEM if n in smem else pltpu.HBM if n in hbm else pltpu.VMEM for n in range(len(args))]
    shapes = [jax.ShapeDtypeStruct(s, t) for s, t in outs]
    out_specs = [
        pl.BlockSpec(memory_space=pltpu.HBM if n in hbm_out else pltpu.VMEM) for n in range(len(outs))
    ]
    if len(outs) == 1:
        shapes, out_specs = shapes[0], out_specs[0]
    moved = sum(a.size * a.dtype.itemsize for a in args)
    return pl.pallas_call(
        inner,
        out_shape=shapes,
        in_specs=[pl.BlockSpec(memory_space=space) for space in spaces],
        out_specs=out_specs,
        scratch_shapes=[pltpu.VMEM(s, t) for s, t in scratch] + [pltpu.SemaphoreType.DMA((n,)) for n in sems],
        compiler_params=pltpu.CompilerParams(vmem_limit_bytes=limit << 20),
        cost_estimate=pl.CostEstimate(flops=flops, bytes_accessed=moved, transcendentals=0),
    )(*args)


def exchange(x, axis):
    return lax.all_to_all(x, axis, split_axis=0, concat_axis=0, tiled=True)


def swap(x):
    return lax.ppermute(x, "core", [(0, 1), (1, 0)])


def on_device(
    pair, cotangent, res_count, w_left, w_left_gate, w_right, w_right_gate, w_gate, w_out
):
    z, g = pair[0], cotangent[0]
    rows, total, _ = z.shape
    pairs = rows // 2
    sides = (w_left, w_left_gate, w_right, w_right_gate)
    mega = 10**6

    blocks = call(
        project_kernel, [((32, 8 * rows, total), BF16)],
        [((4 * C, C), BF16), ((rows, total, C), BF16), ((4, C, C), BF16), ((32, 8 * rows, total), BF16)],
        4000 * mega, res_count, z, *sides, smem=(0,), hbm=(1, 2, 3, 4, 5), hbm_out=(0,), sems=(pairs, 4, pairs),
    )
    factors, w_all = call(
        factors_kernel, [((rows, 4 * C, total), BF16), ((4 * C, C), BF16)], [], 4000 * mega,
        res_count, z, *sides, smem=(0,), after=(blocks,),
    )
    scaled, factor, spread, dnormed = call(
        gates_kernel,
        [((pairs, 2 * C, total), BF16), ((pairs, 2 * C, total), F32), ((2 * C, 2 * C), BF16),
         ((pairs, 2 * C, total), F32)],
        [((C, C), BF16)], 4000 * mega,
        z, g, w_gate, w_out, after=(blocks,),
    )
    blocks = exchange(blocks, DAP)
    edges = call(
        edges_kernel,
        [((32, 4 * rows, total), BF16)],
        [
            ((total // C, 8 * total, C), F32), ((total // C, 4 * total, C), F32),
            ((32, 8 * rows, total), BF16), ((32, 4 * rows, total), BF16),
        ], 4000 * mega,
        blocks, hbm=(0,), hbm_out=(0,), sems=(4, 4), after=(factors, scaled),
    )
    edges = exchange(edges, DAP)
    dedges = call(
        norm_kernel,
        [((32, 4 * rows, total), BF16)],
        [
            ((32, 4 * rows, total), BF16), ((pairs, 2 * C, total), F32), ((32, 4 * rows, total), BF16),
        ], 4000 * mega,
        res_count, edges, dnormed, smem=(0,), hbm=(1, 2), hbm_out=(0,), sems=(rows // 4,) * 3,
    )
    lr = call(
        split_kernel, [((8, total, total), BF16)],
        [((total // C, 8 * total, C), F32), ((32, 8 * rows, total), BF16)], 4000 * mega,
        blocks, hbm=(0,), sems=(4,), after=(dedges,),
    )
    dedges = exchange(dedges, DAP)
    back = call(
        back_kernel,
        [((32, 8 * rows, total), BF16)],
        [
            ((total // C, 4 * total, C), F32), ((total // C, 8 * total, C), F32),
            ((8, total, total), BF16), ((32, 4 * rows, total), BF16), ((32, 8 * rows, total), BF16),
        ], 4000 * mega,
        dedges, lr, hbm=(0, 1), hbm_out=(0,), sems=(4, 4, 4), limit=52,
    )
    dgate, sums = call(
        linear_kernel,
        [((pairs, 2 * C, total), BF16), ((2 * C, C), F32)],
        [((2 * C, 2 * C), BF16), ((pairs, 2 * C, total), BF16), ((C, C), F32), ((2 * C, 2 * C), F32)], 4000 * mega,
        res_count, z, edges, scaled, factor, spread, smem=(0,), after=(back,),
    )
    back = exchange(back, DAP)
    keep, give = call(
        weights_kernel,
        [((3 * C, C), F32), ((3 * C, C), F32)],
        [
            ((6 * C, C), F32), ((4 * C, C), F32), ((rows, total, C), BF16),
            ((32, 8 * rows, total), BF16), ((rows, 4 * C, total), BF16),
        ], 4000 * mega,
        z, back, factors, sums, hbm=(0, 1, 2, 3), sems=(pairs, pairs, pairs, 1),
    )
    share = exchange((keep + swap(give)).reshape(16, 24, C), ("x", "y")).sum(axis=0, keepdims=True)
    share = exchange(jnp.broadcast_to(share, (8, 24, C)), "z").sum(axis=0, keepdims=True)
    share = jnp.broadcast_to(share, (16, 24, C))
    grad = call(
        pair_kernel,
        [((1, rows, total, C), BF16)],
        [((C, 4 * C), BF16)], 4000 * mega,
        back, factors, dgate, w_all, w_gate, after=(share,),
    )
    mine, grad = lax.optimization_barrier((exchange(share, ("x", "y")), grad))
    mine = mine.reshape(3, C, C)
    other = swap(mine)
    first = lax.axis_index("core") == 0
    whole = [jnp.where(first, mine[n], other[n]) for n in range(3)]
    whole += [jnp.where(first, other[n], mine[n]) for n in range(3)]
    return (grad, *whole)


def solution(mesh):
    chips = Mesh(mesh.devices.reshape(4, 2, 8, 4), ISLAND + DAP)
    rows = P(ISLAND, DAP, None, None)
    return jax.shard_map(
        on_device,
        mesh=chips,
        in_specs=(rows, rows, P(ISLAND), P(), P(), P(), P(), P(), P()),
        out_specs=(rows, P(), P(), P(), P(), P(), P()),
        check_vma=False,
    )
```

```python
import jax
import jax.numpy as jnp
from jax import lax
from jax.experimental import pallas as pl
from jax.experimental.pallas import tpu as pltpu
from jax.sharding import Mesh
from jax.sharding import PartitionSpec as P

F32 = jnp.float32
BF16 = jnp.bfloat16
C = 128
HI = lax.Precision.HIGHEST
ISLAND, DAP = ("x", "core"), ("z", "y")


def dot(a, b, ca, cb, precision=None):
    return lax.dot_general(
        a, b, (((ca,), (cb,)), ((), ())), preferred_element_type=F32, precision=precision
    )


def iota(shape, dim):
    return lax.broadcasted_iota(jnp.int32, shape, dim)


def pick(side):
    row, chan = iota((2 * C, C), 0), iota((2 * C, C), 1)
    hit = ((row % 8) // 4 == side) & (chan == (row // 8) * 4 + row % 4)
    return hit.astype(F32)


def spread_rows(w_out):
    parts = [dot(pick(side).astype(BF16), w_out, 1, 0) for side in range(2)]
    return jnp.concatenate(parts, axis=1).astype(BF16)


def both_projections(w_left, w_left_gate, w_right, w_right_gate):
    on_left, on_right = pick(0).astype(BF16), pick(1).astype(BF16)
    proj = dot(on_left, w_left, 1, 1) + dot(on_right, w_right, 1, 1)
    gate = dot(on_left, w_left_gate, 1, 1) + dot(on_right, w_right_gate, 1, 1)
    return jnp.concatenate([proj, gate], axis=0).astype(BF16)


def row_mask(count, row, shape):
    return jnp.where((row < count) & (iota(shape, len(shape) - 1) < count), 1.0, 0.0)


def first_row(rows):
    return lax.axis_index(DAP) * rows


def each(n, step):
    def body(m, carry):
        step(m)
        return carry

    lax.fori_loop(0, n, body, 0)


def two(m):
    return pl.ds(2 * m, 2)


def tile(m):
    return pl.ds(pl.multiple_of(16 * m, 16), 16)


def project_kernel(
    count_ref, z_hbm, wl_hbm, wlg_hbm, wr_hbm, wrg_hbm, out_hbm,
    w_ref, z_ref, side_ref, out_ref, z_sem, w_sem, out_sem,
):
    rows, total, _ = z_ref.shape
    count = count_ref[0]
    start = first_row(rows)
    sides = [
        pltpu.make_async_copy(ref, side_ref.at[n], w_sem.at[n])
        for n, ref in enumerate((wl_hbm, wlg_hbm, wr_hbm, wrg_hbm))
    ]
    for copy in sides:
        copy.start()

    def cells(m):
        return pltpu.make_async_copy(z_hbm.at[two(m)], z_ref.at[two(m)], z_sem.at[m])

    def sent(m):
        return pltpu.make_async_copy(out_ref.at[:, tile(m)], out_hbm.at[:, tile(m)], out_sem.at[m])

    each(rows // 2, lambda m: cells(m).start())
    for copy in sides:
        copy.wait()
    w_ref[...] = both_projections(side_ref[0], side_ref[1], side_ref[2], side_ref[3])

    def step(m):
        cells(m).wait()
        halves = []
        for h in range(2):
            i = 2 * m + h
            pg = dot(w_ref[...], z_ref[i], 1, 1)
            mask = row_mask(count, start + i, (1, total))
            made = mask * jax.nn.sigmoid(pg[2 * C :]) * pg[: 2 * C]
            halves.append(made.reshape(32, 8, total))
        out_ref[:, tile(m), :] = jnp.concatenate(halves, axis=1).astype(BF16)
        sent(m).start()

    each(rows // 2, step)
    each(rows // 2, lambda m: sent(m).wait())


def factors_kernel(count_ref, z_ref, wl_ref, wlg_ref, wr_ref, wrg_ref, out_ref, w_ref):
    rows, total, _ = z_ref.shape
    count = count_ref[0]
    start = first_row(rows)
    w_ref[...] = both_projections(wl_ref[...], wlg_ref[...], wr_ref[...], wrg_ref[...])

    def body(i, carry):
        pg = dot(w_ref[...], z_ref[i], 1, 1)
        gate = jax.nn.sigmoid(pg[2 * C :])
        masked = gate * row_mask(count, start + i, (1, total))
        out_ref[i, : 2 * C, :] = masked.astype(BF16)
        out_ref[i, 2 * C :, :] = (masked * pg[: 2 * C] * (1.0 - gate)).astype(BF16)
        return carry

    lax.fori_loop(0, rows, body, 0)


def put_wide(ref, at, rows, value):
    for n in range(ref.shape[0]):
        ref[n, pl.ds(at, rows), :] = value[:, n * C : (n + 1) * C]


def take(ref, first, count, step):
    return jnp.concatenate(
        [ref[n, pl.ds(first, count, stride=step), :] for n in range(ref.shape[0])], axis=1
    )


def put(ref, first, count, step, value):
    for n in range(ref.shape[0]):
        ref[n, pl.ds(first, count, stride=step), :] = value[:, n * C : (n + 1) * C]


def get_rows(ref, at, rows):
    return jnp.concatenate([ref[n, pl.ds(at, rows), :] for n in range(ref.shape[0])], axis=1)


def widen_all(x_hbm, x_ref, wide_ref, sem):
    devices, block, _ = x_ref.shape
    part = devices // 4

    def copy(n):
        here = pl.ds(n * part, part)
        return pltpu.make_async_copy(x_hbm.at[here], x_ref.at[here], sem.at[n])

    def widen(s):
        put_wide(wide_ref, pl.multiple_of(s * block, block), block, x_ref[s].astype(F32))

    def step(n):
        copy(n).wait()
        each(part, lambda s: widen(n * part + s))

    return lambda: each(4, lambda n: copy(n).start()), lambda: each(4, step)


def edges_kernel(x_hbm, out_hbm, wide_ref, prod_ref, x_ref, out_ref, x_sem, out_sem):
    total = x_ref.shape[2]
    fetch, widen = widen_all(x_hbm, x_ref, wide_ref, x_sem)
    fetch()
    widen()
    for c in range(4):
        left = take(wide_ref, c, total, 8).astype(BF16)
        right = take(wide_ref, 4 + c, total, 8).astype(BF16)
        put(prod_ref, c, total, 4, dot(left, right, 1, 1))
    for copy in narrowed(prod_ref, out_ref, out_hbm, out_sem):
        copy.wait()


def split_kernel(x_hbm, out_ref, wide_ref, x_ref, x_sem):
    total = x_ref.shape[2]
    fetch, widen = widen_all(x_hbm, x_ref, wide_ref, x_sem)
    fetch()
    widen()
    for c in range(4):
        out_ref[2 * c] = take(wide_ref, c, total, 8).astype(BF16)
        out_ref[2 * c + 1] = take(wide_ref, 4 + c, total, 8).astype(BF16)


def narrowed(prod_ref, out_ref, out_hbm, sem):
    devices, block, _ = out_ref.shape
    part = devices // 4
    copies = []
    for n in range(4):

        def narrow(s, carry):
            at = pl.multiple_of(s * block, block)
            out_ref[s] = get_rows(prod_ref, at, block).astype(BF16)
            return carry

        lax.fori_loop(n * part, (n + 1) * part, narrow, 0)
        here = pl.ds(n * part, part)
        copies.append(pltpu.make_async_copy(out_ref.at[here], out_hbm.at[here], sem.at[n]))
        copies[-1].start()
    return copies


def gates_kernel(z_ref, g_ref, wg_ref, wo_ref, ds_ref, fac_ref, wx_ref, dn_ref, wgt_ref):
    rows = z_ref.shape[0]
    wgt_ref[...] = wg_ref[...].astype(F32).T.astype(BF16)
    wx_ref[...] = spread_rows(wo_ref[...])

    def body(m, carry):
        for h in range(2):
            i = 2 * m + h
            gate = jax.nn.sigmoid(dot(wgt_ref[...], z_ref[i], 1, 1))
            scaled = g_ref[i].astype(F32).T * gate
            ds_ref[m, h * C : (h + 1) * C, :] = scaled.astype(BF16)
            fac_ref[m, h * C : (h + 1) * C, :] = scaled * (1.0 - gate)
        dn_ref[m] = dot(wx_ref[...], ds_ref[m], 1, 0)
        return carry

    lax.fori_loop(0, rows // 2, body, 0)


def chan_mean(x):
    s = jnp.sum(x, axis=0)
    top = iota(s.shape, 0) < 4
    first = jnp.sum(jnp.where(top, s, 0.0), axis=0, keepdims=True)
    second = jnp.sum(jnp.where(top, 0.0, s), axis=0, keepdims=True)
    return jnp.where(top, first, second) * (1.0 / C)


def standard(e):
    shifted = e - chan_mean(e)[None]
    rs = lax.rsqrt(chan_mean(shifted * shifted) + 1e-05)
    return shifted * rs[None], rs


def cell_mask(count, row, total):
    return row_mask(count, row + iota((8, total), 0) // 4, (8, total))


def norm_kernel(count_ref, e_hbm, dn_hbm, de_hbm, e_ref, dn_ref, de_ref, e_sem, dn_sem, de_sem):
    devices, block, total = e_ref.shape
    rows = block // 4
    count = count_ref[0]
    start = first_row(rows)

    def came(q):
        return (
            pltpu.make_async_copy(e_hbm.at[:, tile(q)], e_ref.at[:, tile(q)], e_sem.at[q]),
            pltpu.make_async_copy(dn_hbm.at[two(q)], dn_ref.at[two(q)], dn_sem.at[q]),
        )

    def gone(q):
        return pltpu.make_async_copy(de_ref.at[:, tile(q)], de_hbm.at[:, tile(q)], de_sem.at[q])

    def begin(q):
        for copy in came(q):
            copy.start()

    def step(q):
        for copy in came(q):
            copy.wait()
        e_all = e_ref[:, tile(q), :].astype(F32)
        halves = []
        for h in range(2):
            xhat, rs = standard(e_all[:, 8 * h : 8 * h + 8, :])
            mask = cell_mask(count, start + 4 * q + 2 * h, total)
            dn = dn_ref[2 * q + h].reshape(32, 8, total)
            m1 = chan_mean(dn)
            m2 = chan_mean(dn * xhat)
            halves.append((mask * rs)[None] * (dn - m1[None] - xhat * m2[None]))
        de_ref[:, tile(q), :] = jnp.concatenate(halves, axis=1).astype(BF16)
        gone(q).start()

    each(rows // 4, begin)
    each(rows // 4, step)
    each(rows // 4, lambda q: gone(q).wait())


def linear_kernel(count_ref, z_ref, e_ref, ds_ref, fac_ref, wx_in_ref, dg_ref, sums_ref, wx_ref, nm_ref, ga_ref, oa_ref):
    rows, total, _ = z_ref.shape
    count = count_ref[0]
    start = first_row(rows)

    def normalize(q):
        e_all = e_ref[:, tile(q), :].astype(F32)
        for h in range(2):
            xhat, _ = standard(e_all[:, 8 * h : 8 * h + 8, :])
            mask = cell_mask(count, start + 4 * q + 2 * h, total)
            nm_ref[2 * q + h] = (xhat * mask[None]).reshape(2 * C, total).astype(BF16)

    each(rows // 4, normalize)
    wx_ref[...] = wx_in_ref[...].astype(F32).T.astype(BF16)
    ga_ref[...] = jnp.zeros_like(ga_ref)
    oa_ref[...] = jnp.zeros_like(oa_ref)

    def body(m, carry):
        lin = dot(wx_ref[...], nm_ref[m], 1, 0)
        dg_ref[m] = (lin * fac_ref[m]).astype(BF16)
        for h in range(2):
            ga_ref[...] += dot(dg_ref[m, h * C : (h + 1) * C, :], z_ref[2 * m + h], 1, 0)
        oa_ref[...] += dot(nm_ref[m], ds_ref[m], 1, 1)
        return carry

    lax.fori_loop(0, rows // 2, body, 0)
    sums_ref[:C, :] = ga_ref[...].T
    sums_ref[C:, :] = dot(pick(0), oa_ref[:, :C], 0, 0, HI) + dot(pick(1), oa_ref[:, C:], 0, 0, HI)


def back_kernel(x_hbm, lr_hbm, out_hbm, wide_ref, prod_ref, lr_ref, x_ref, out_ref, lr_sem, x_sem, out_sem):
    total = x_ref.shape[2]

    def kept(c):
        return pltpu.make_async_copy(lr_hbm.at[two(c)], lr_ref.at[two(c)], lr_sem.at[c])

    fetch, widen = widen_all(x_hbm, x_ref, wide_ref, x_sem)
    fetch()
    each(4, lambda c: kept(c).start())
    widen()
    for c in range(4):
        de = take(wide_ref, c, total, 4).astype(BF16)
        kept(c).wait()
        put(prod_ref, c, total, 8, dot(de, lr_ref[2 * c + 1], 1, 0))
        put(prod_ref, 4 + c, total, 8, dot(de, lr_ref[2 * c], 0, 0))
    for copy in narrowed(prod_ref, out_ref, out_hbm, out_sem):
        copy.wait()


def by_side(x):
    x = x.reshape(16, 2, 8, C)
    even, odd = x[:, 0], x[:, 1]
    top = iota((16, 8, C), 1) < 4
    left = jnp.where(top, even, pltpu.roll(odd, 4, 1))
    right = jnp.where(top, pltpu.roll(even, 4, 1), odd)
    return left.reshape(C, C), right.reshape(C, C)


def side_gradients(d_ref, fac_ref, m, h):
    d = d_ref[:, tile(m), :].astype(F32)[:, 8 * h : 8 * h + 8, :].reshape(2 * C, -1)
    factor = fac_ref[2 * m + h].astype(F32)
    return jnp.concatenate([d * factor[: 2 * C], d * factor[2 * C :]], axis=0).astype(BF16)


def weights_kernel(
    z_hbm, d_hbm, fac_hbm, sums_hbm, keep_ref, give_ref, out_ref, acc_ref, z_ref, d_ref, fac_ref,
    z_sem, d_sem, fac_sem, sums_sem,
):
    rows, total, _ = z_ref.shape

    def came(m):
        return (
            pltpu.make_async_copy(d_hbm.at[:, tile(m)], d_ref.at[:, tile(m)], d_sem.at[m]),
            pltpu.make_async_copy(fac_hbm.at[two(m)], fac_ref.at[two(m)], fac_sem.at[m]),
            pltpu.make_async_copy(z_hbm.at[two(m)], z_ref.at[two(m)], z_sem.at[m]),
        )

    def begin(m):
        for copy in came(m):
            copy.start()

    def step(m):
        for copy in came(m):
            copy.wait()
        made = jnp.concatenate([side_gradients(d_ref, fac_ref, m, h) for h in range(2)], axis=1)
        acc_ref[...] += dot(made, z_ref[two(m)].reshape(2 * total, C), 1, 0)

    each(rows // 2, begin)
    rest = pltpu.make_async_copy(sums_hbm, out_ref.at[pl.ds(4 * C, 2 * C)], sums_sem.at[0])
    rest.start()
    acc_ref[...] = jnp.zeros_like(acc_ref)
    each(rows // 2, step)
    for n in range(2):
        left, right = by_side(acc_ref[2 * C * n : 2 * C * (n + 1), :])
        out_ref[n * C : (n + 1) * C, :] = left.T
        out_ref[(2 + n) * C : (3 + n) * C, :] = right.T
    rest.wait()
    half = 3 * C
    keep = pl.multiple_of(lax.axis_index("core") * half, half)
    keep_ref[...] = out_ref[pl.ds(keep, half), :]
    give_ref[...] = out_ref[pl.ds(half - keep, half), :]


def pair_kernel(d_ref, fac_ref, dg_ref, w_ref, wg_ref, out_ref, wt_ref):
    rows = fac_ref.shape[0]
    wt_ref[...] = w_ref[...].astype(F32).T.astype(BF16)

    def body(m, carry):
        for h in range(2):
            i = 2 * m + h
            made = dot(wt_ref[...], side_gradients(d_ref, fac_ref, m, h), 1, 0)
            made += dot(wg_ref[...], dg_ref[m, h * C : (h + 1) * C, :], 1, 0)
            out_ref[0, i] = made.T.astype(BF16)
        return carry

    lax.fori_loop(0, rows // 2, body, 0)


def call(body, outs, scratch, flops, *args, smem=(), hbm=(), hbm_out=(), sems=(), after=(), limit=62):
    given = len(args)
    args = (*args, *after)
    hbm = (*hbm, *range(given, len(args)))

    def inner(*refs):
        body(*refs[:given], *refs[given + len(after) :])

    spaces = [pltpu.SMEM if n in smem else pltpu.HBM if n in hbm else pltpu.VMEM for n in range(len(args))]
    shapes = [jax.ShapeDtypeStruct(s, t) for s, t in outs]
    out_specs = [
        pl.BlockSpec(memory_space=pltpu.HBM if n in hbm_out else pltpu.VMEM) for n in range(len(outs))
    ]
    if len(outs) == 1:
        shapes, out_specs = shapes[0], out_specs[0]
    moved = sum(a.size * a.dtype.itemsize for a in args)
    return pl.pallas_call(
        inner,
        out_shape=shapes,
        in_specs=[pl.BlockSpec(memory_space=space) for space in spaces],
        out_specs=out_specs,
        scratch_shapes=[pltpu.VMEM(s, t) for s, t in scratch] + [pltpu.SemaphoreType.DMA((n,)) for n in sems],
        compiler_params=pltpu.CompilerParams(vmem_limit_bytes=limit << 20),
        cost_estimate=pl.CostEstimate(flops=flops, bytes_accessed=moved, transcendentals=0),
    )(*args)


def exchange(x, axis):
    return lax.all_to_all(x, axis, split_axis=0, concat_axis=0, tiled=True)


def swap(x):
    return lax.ppermute(x, "core", [(0, 1), (1, 0)])


def on_device(
    pair, cotangent, res_count, w_left, w_left_gate, w_right, w_right_gate, w_gate, w_out
):
    z, g = pair[0], cotangent[0]
    rows, total, _ = z.shape
    pairs = rows // 2
    sides = (w_left, w_left_gate, w_right, w_right_gate)
    mega = 10**6

    blocks = call(
        project_kernel, [((32, 8 * rows, total), BF16)],
        [((4 * C, C), BF16), ((rows, total, C), BF16), ((4, C, C), BF16), ((32, 8 * rows, total), BF16)],
        4000 * mega, res_count, z, *sides, smem=(0,), hbm=(1, 2, 3, 4, 5), hbm_out=(0,), sems=(pairs, 4, pairs),
    )
    factors, w_all = call(
        factors_kernel, [((rows, 4 * C, total), BF16), ((4 * C, C), BF16)], [], 4000 * mega,
        res_count, z, *sides, smem=(0,), after=(blocks,),
    )
    scaled, factor, spread, dnormed = call(
        gates_kernel,
        [((pairs, 2 * C, total), BF16), ((pairs, 2 * C, total), F32), ((2 * C, 2 * C), BF16),
         ((pairs, 2 * C, total), F32)],
        [((C, C), BF16)], 4000 * mega,
        z, g, w_gate, w_out, after=(blocks,),
    )
    blocks = exchange(blocks, DAP)
    edges = call(
        edges_kernel,
        [((32, 4 * rows, total), BF16)],
        [
            ((total // C, 8 * total, C), F32), ((total // C, 4 * total, C), F32),
            ((32, 8 * rows, total), BF16), ((32, 4 * rows, total), BF16),
        ], 4000 * mega,
        blocks, hbm=(0,), hbm_out=(0,), sems=(4, 4), after=(factors, scaled),
    )
    edges = exchange(edges, DAP)
    dedges = call(
        norm_kernel,
        [((32, 4 * rows, total), BF16)],
        [
            ((32, 4 * rows, total), BF16), ((pairs, 2 * C, total), F32), ((32, 4 * rows, total), BF16),
        ], 4000 * mega,
        res_count, edges, dnormed, smem=(0,), hbm=(1, 2), hbm_out=(0,), sems=(rows // 4,) * 3,
    )
    lr = call(
        split_kernel, [((8, total, total), BF16)],
        [((total // C, 8 * total, C), F32), ((32, 8 * rows, total), BF16)], 4000 * mega,
        blocks, hbm=(0,), sems=(4,), after=(dedges,),
    )
    dedges = exchange(dedges, DAP)
    back = call(
        back_kernel,
        [((32, 8 * rows, total), BF16)],
        [
            ((total // C, 4 * total, C), F32), ((total // C, 8 * total, C), F32),
            ((8, total, total), BF16), ((32, 4 * rows, total), BF16), ((32, 8 * rows, total), BF16),
        ], 4000 * mega,
        dedges, lr, hbm=(0, 1), hbm_out=(0,), sems=(4, 4, 4), limit=52,
    )
    dgate, sums = call(
        linear_kernel,
        [((pairs, 2 * C, total), BF16), ((2 * C, C), F32)],
        [((2 * C, 2 * C), BF16), ((pairs, 2 * C, total), BF16), ((C, C), F32), ((2 * C, 2 * C), F32)], 4000 * mega,
        res_count, z, edges, scaled, factor, spread, smem=(0,), after=(back,),
    )
    back = exchange(back, DAP)
    keep, give = call(
        weights_kernel,
        [((3 * C, C), F32), ((3 * C, C), F32)],
        [
            ((6 * C, C), F32), ((4 * C, C), F32), ((rows, total, C), BF16),
            ((32, 8 * rows, total), BF16), ((rows, 4 * C, total), BF16),
        ], 4000 * mega,
        z, back, factors, sums, hbm=(0, 1, 2, 3), sems=(pairs, pairs, pairs, 1), limit=50,
    )
    share = exchange((keep + swap(give)).reshape(16, 24, C), ("x", "y")).sum(axis=0, keepdims=True)
    share = exchange(jnp.broadcast_to(share, (8, 24, C)), "z").sum(axis=0, keepdims=True)
    share = jnp.broadcast_to(share, (16, 24, C))
    grad = call(
        pair_kernel,
        [((1, rows, total, C), BF16)],
        [((C, 4 * C), BF16)], 4000 * mega,
        back, factors, dgate, w_all, w_gate, after=(share,), limit=50,
    )
    mine, grad = lax.optimization_barrier((exchange(share, ("x", "y")), grad))
    mine = mine.reshape(3, C, C)
    other = swap(mine)
    first = lax.axis_index("core") == 0
    whole = [jnp.where(first, mine[n], other[n]) for n in range(3)]
    whole += [jnp.where(first, other[n], mine[n]) for n in range(3)]
    return (grad, *whole)


def solution(mesh):
    chips = Mesh(mesh.devices.reshape(4, 2, 8, 4), ISLAND + DAP)
    rows = P(ISLAND, DAP, None, None)
    return jax.shard_map(
        on_device,
        mesh=chips,
        in_specs=(rows, rows, P(ISLAND), P(), P(), P(), P(), P(), P()),
        out_specs=(rows, P(), P(), P(), P(), P(), P()),
        check_vma=False,
    )
```

```python
import jax
import jax.numpy as jnp
from jax import lax
from jax.experimental import pallas as pl
from jax.experimental.pallas import tpu as pltpu
from jax.sharding import Mesh
from jax.sharding import PartitionSpec as P

F32 = jnp.float32
BF16 = jnp.bfloat16
C = 128
HI = lax.Precision.HIGHEST
ISLAND, DAP = ("x", "core"), ("z", "y")


def dot(a, b, ca, cb, precision=None):
    return lax.dot_general(
        a, b, (((ca,), (cb,)), ((), ())), preferred_element_type=F32, precision=precision
    )


def iota(shape, dim):
    return lax.broadcasted_iota(jnp.int32, shape, dim)


def pick(side):
    row, chan = iota((2 * C, C), 0), iota((2 * C, C), 1)
    hit = ((row % 8) // 4 == side) & (chan == (row // 8) * 4 + row % 4)
    return hit.astype(F32)


def spread_rows(w_out):
    parts = [dot(pick(side).astype(BF16), w_out, 1, 0) for side in range(2)]
    return jnp.concatenate(parts, axis=1).astype(BF16)


def both_projections(w_left, w_left_gate, w_right, w_right_gate):
    on_left, on_right = pick(0).astype(BF16), pick(1).astype(BF16)
    proj = dot(on_left, w_left, 1, 1) + dot(on_right, w_right, 1, 1)
    gate = dot(on_left, w_left_gate, 1, 1) + dot(on_right, w_right_gate, 1, 1)
    return jnp.concatenate([proj, gate], axis=0).astype(BF16)


def row_mask(count, row, shape):
    return jnp.where((row < count) & (iota(shape, len(shape) - 1) < count), 1.0, 0.0)


def first_row(rows):
    return lax.axis_index(DAP) * rows


def each(n, step):
    def body(m, carry):
        step(m)
        return carry

    lax.fori_loop(0, n, body, 0)


def two(m):
    return pl.ds(2 * m, 2)


def tile(m):
    return pl.ds(pl.multiple_of(16 * m, 16), 16)


def project_kernel(
    count_ref, z_hbm, wl_hbm, wlg_hbm, wr_hbm, wrg_hbm, out_hbm,
    w_ref, z_ref, side_ref, out_ref, z_sem, w_sem, out_sem,
):
    rows, total, _ = z_ref.shape
    count = count_ref[0]
    start = first_row(rows)
    sides = [
        pltpu.make_async_copy(ref, side_ref.at[n], w_sem.at[n])
        for n, ref in enumerate((wl_hbm, wlg_hbm, wr_hbm, wrg_hbm))
    ]
    for copy in sides:
        copy.start()

    def cells(m):
        return pltpu.make_async_copy(z_hbm.at[two(m)], z_ref.at[two(m)], z_sem.at[m])

    def sent(m):
        return pltpu.make_async_copy(out_ref.at[:, tile(m)], out_hbm.at[:, tile(m)], out_sem.at[m])

    each(rows // 2, lambda m: cells(m).start())
    for copy in sides:
        copy.wait()
    w_ref[...] = both_projections(side_ref[0], side_ref[1], side_ref[2], side_ref[3])

    def step(m):
        cells(m).wait()
        halves = []
        for h in range(2):
            i = 2 * m + h
            pg = dot(w_ref[...], z_ref[i], 1, 1)
            mask = row_mask(count, start + i, (1, total))
            made = mask * jax.nn.sigmoid(pg[2 * C :]) * pg[: 2 * C]
            halves.append(made.reshape(32, 8, total))
        out_ref[:, tile(m), :] = jnp.concatenate(halves, axis=1).astype(BF16)
        sent(m).start()

    each(rows // 2, step)
    each(rows // 2, lambda m: sent(m).wait())


def factors_kernel(count_ref, z_ref, wl_ref, wlg_ref, wr_ref, wrg_ref, out_ref, w_ref):
    rows, total, _ = z_ref.shape
    count = count_ref[0]
    start = first_row(rows)
    w_ref[...] = both_projections(wl_ref[...], wlg_ref[...], wr_ref[...], wrg_ref[...])

    def body(i, carry):
        pg = dot(w_ref[...], z_ref[i], 1, 1)
        gate = jax.nn.sigmoid(pg[2 * C :])
        masked = gate * row_mask(count, start + i, (1, total))
        out_ref[i, : 2 * C, :] = masked.astype(BF16)
        out_ref[i, 2 * C :, :] = (masked * pg[: 2 * C] * (1.0 - gate)).astype(BF16)
        return carry

    lax.fori_loop(0, rows, body, 0)


def put_wide(ref, at, rows, value):
    for n in range(ref.shape[0]):
        ref[n, pl.ds(at, rows), :] = value[:, n * C : (n + 1) * C]


def take(ref, first, count, step):
    return jnp.concatenate(
        [ref[n, pl.ds(first, count, stride=step), :] for n in range(ref.shape[0])], axis=1
    )


def put(ref, first, count, step, value):
    for n in range(ref.shape[0]):
        ref[n, pl.ds(first, count, stride=step), :] = value[:, n * C : (n + 1) * C]


def get_rows(ref, at, rows):
    return jnp.concatenate([ref[n, pl.ds(at, rows), :] for n in range(ref.shape[0])], axis=1)


def widen_all(x_hbm, x_ref, wide_ref, sem):
    devices, block, _ = x_ref.shape
    part = devices // 4

    def copy(n):
        here = pl.ds(n * part, part)
        return pltpu.make_async_copy(x_hbm.at[here], x_ref.at[here], sem.at[n])

    def widen(s):
        put_wide(wide_ref, pl.multiple_of(s * block, block), block, x_ref[s].astype(F32))

    def step(n):
        copy(n).wait()
        each(part, lambda s: widen(n * part + s))

    return lambda: each(4, lambda n: copy(n).start()), lambda: each(4, step)


def edges_kernel(x_hbm, out_hbm, wide_ref, prod_ref, x_ref, out_ref, x_sem, out_sem):
    total = x_ref.shape[2]
    fetch, widen = widen_all(x_hbm, x_ref, wide_ref, x_sem)
    fetch()
    widen()
    for c in range(4):
        left = take(wide_ref, c, total, 8).astype(BF16)
        right = take(wide_ref, 4 + c, total, 8).astype(BF16)
        put(prod_ref, c, total, 4, dot(left, right, 1, 1))
    for copy in narrowed(prod_ref, out_ref, out_hbm, out_sem):
        copy.wait()


def split_kernel(x_hbm, out_ref, wide_ref, x_ref, x_sem):
    total = x_ref.shape[2]
    fetch, widen = widen_all(x_hbm, x_ref, wide_ref, x_sem)
    fetch()
    widen()
    for c in range(4):
        out_ref[2 * c] = take(wide_ref, c, total, 8).astype(BF16)
        out_ref[2 * c + 1] = take(wide_ref, 4 + c, total, 8).astype(BF16)


def narrowed(prod_ref, out_ref, out_hbm, sem):
    devices, block, _ = out_ref.shape
    part = devices // 4
    copies = []
    for n in range(4):

        def narrow(s, carry):
            at = pl.multiple_of(s * block, block)
            out_ref[s] = get_rows(prod_ref, at, block).astype(BF16)
            return carry

        lax.fori_loop(n * part, (n + 1) * part, narrow, 0)
        here = pl.ds(n * part, part)
        copies.append(pltpu.make_async_copy(out_ref.at[here], out_hbm.at[here], sem.at[n]))
        copies[-1].start()
    return copies


def gates_kernel(z_ref, g_ref, wg_ref, wo_ref, ds_ref, fac_ref, wx_ref, dn_ref, wgt_ref):
    rows = z_ref.shape[0]
    wgt_ref[...] = wg_ref[...].astype(F32).T.astype(BF16)
    wx_ref[...] = spread_rows(wo_ref[...])

    def body(m, carry):
        for h in range(2):
            i = 2 * m + h
            gate = jax.nn.sigmoid(dot(wgt_ref[...], z_ref[i], 1, 1))
            scaled = g_ref[i].astype(F32).T * gate
            ds_ref[m, h * C : (h + 1) * C, :] = scaled.astype(BF16)
            fac_ref[m, h * C : (h + 1) * C, :] = scaled * (1.0 - gate)
        dn_ref[m] = dot(wx_ref[...], ds_ref[m], 1, 0)
        return carry

    lax.fori_loop(0, rows // 2, body, 0)


def chan_mean(x):
    s = jnp.sum(x, axis=0)
    top = iota(s.shape, 0) < 4
    first = jnp.sum(jnp.where(top, s, 0.0), axis=0, keepdims=True)
    second = jnp.sum(jnp.where(top, 0.0, s), axis=0, keepdims=True)
    return jnp.where(top, first, second) * (1.0 / C)


def standard(e):
    shifted = e - chan_mean(e)[None]
    rs = lax.rsqrt(chan_mean(shifted * shifted) + 1e-05)
    return shifted * rs[None], rs


def cell_mask(count, row, total):
    return row_mask(count, row + iota((8, total), 0) // 4, (8, total))


def norm_kernel(count_ref, e_hbm, dn_hbm, de_hbm, e_ref, dn_ref, de_ref, e_sem, dn_sem, de_sem):
    devices, block, total = e_ref.shape
    rows = block // 4
    count = count_ref[0]
    start = first_row(rows)

    def came(q):
        return (
            pltpu.make_async_copy(e_hbm.at[:, tile(q)], e_ref.at[:, tile(q)], e_sem.at[q]),
            pltpu.make_async_copy(dn_hbm.at[two(q)], dn_ref.at[two(q)], dn_sem.at[q]),
        )

    def gone(q):
        return pltpu.make_async_copy(de_ref.at[:, tile(q)], de_hbm.at[:, tile(q)], de_sem.at[q])

    def begin(q):
        for copy in came(q):
            copy.start()

    def step(q):
        for copy in came(q):
            copy.wait()
        e_all = e_ref[:, tile(q), :].astype(F32)
        halves = []
        for h in range(2):
            xhat, rs = standard(e_all[:, 8 * h : 8 * h + 8, :])
            mask = cell_mask(count, start + 4 * q + 2 * h, total)
            dn = dn_ref[2 * q + h].reshape(32, 8, total)
            m1 = chan_mean(dn)
            m2 = chan_mean(dn * xhat)
            halves.append((mask * rs)[None] * (dn - m1[None] - xhat * m2[None]))
        de_ref[:, tile(q), :] = jnp.concatenate(halves, axis=1).astype(BF16)
        gone(q).start()

    each(rows // 4, begin)
    each(rows // 4, step)
    each(rows // 4, lambda q: gone(q).wait())


def linear_kernel(count_ref, z_ref, e_ref, ds_ref, fac_ref, wx_in_ref, dg_ref, sums_ref, wx_ref, nm_ref, ga_ref, oa_ref):
    rows, total, _ = z_ref.shape
    count = count_ref[0]
    start = first_row(rows)

    def normalize(q):
        e_all = e_ref[:, tile(q), :].astype(F32)
        for h in range(2):
            xhat, _ = standard(e_all[:, 8 * h : 8 * h + 8, :])
            mask = cell_mask(count, start + 4 * q + 2 * h, total)
            nm_ref[2 * q + h] = (xhat * mask[None]).reshape(2 * C, total).astype(BF16)

    each(rows // 4, normalize)
    wx_ref[...] = wx_in_ref[...].astype(F32).T.astype(BF16)
    ga_ref[...] = jnp.zeros_like(ga_ref)
    oa_ref[...] = jnp.zeros_like(oa_ref)

    def body(m, carry):
        lin = dot(wx_ref[...], nm_ref[m], 1, 0)
        dg_ref[m] = (lin * fac_ref[m]).astype(BF16)
        for h in range(2):
            ga_ref[...] += dot(dg_ref[m, h * C : (h + 1) * C, :], z_ref[2 * m + h], 1, 0)
        oa_ref[...] += dot(nm_ref[m], ds_ref[m], 1, 1)
        return carry

    lax.fori_loop(0, rows // 2, body, 0)
    sums_ref[:C, :] = ga_ref[...].T
    sums_ref[C:, :] = dot(pick(0), oa_ref[:, :C], 0, 0, HI) + dot(pick(1), oa_ref[:, C:], 0, 0, HI)


def back_kernel(x_hbm, lr_hbm, out_hbm, wide_ref, prod_ref, lr_ref, x_ref, out_ref, lr_sem, x_sem, out_sem):
    total = x_ref.shape[2]

    def kept(c):
        return pltpu.make_async_copy(lr_hbm.at[two(c)], lr_ref.at[two(c)], lr_sem.at[c])

    fetch, widen = widen_all(x_hbm, x_ref, wide_ref, x_sem)
    fetch()
    each(4, lambda c: kept(c).start())
    widen()
    for c in range(4):
        de = take(wide_ref, c, total, 4).astype(BF16)
        kept(c).wait()
        put(prod_ref, c, total, 8, dot(de, lr_ref[2 * c + 1], 1, 0))
        put(prod_ref, 4 + c, total, 8, dot(de, lr_ref[2 * c], 0, 0))
    for copy in narrowed(prod_ref, out_ref, out_hbm, out_sem):
        copy.wait()


def by_side(x):
    x = x.reshape(16, 2, 8, C)
    even, odd = x[:, 0], x[:, 1]
    top = iota((16, 8, C), 1) < 4
    left = jnp.where(top, even, pltpu.roll(odd, 4, 1))
    right = jnp.where(top, pltpu.roll(even, 4, 1), odd)
    return left.reshape(C, C), right.reshape(C, C)


def side_gradients(d_ref, fac_ref, m, h):
    d = d_ref[:, tile(m), :].astype(F32)[:, 8 * h : 8 * h + 8, :].reshape(2 * C, -1)
    factor = fac_ref[2 * m + h].astype(F32)
    return jnp.concatenate([d * factor[: 2 * C], d * factor[2 * C :]], axis=0).astype(BF16)


def weights_kernel(
    z_hbm, d_hbm, fac_hbm, sums_hbm, keep_ref, give_ref, out_ref, acc_ref, z_ref, d_ref, fac_ref,
    z_sem, d_sem, fac_sem, sums_sem,
):
    rows, total, _ = z_ref.shape

    def came(m):
        return (
            pltpu.make_async_copy(d_hbm.at[:, tile(m)], d_ref.at[:, tile(m)], d_sem.at[m]),
            pltpu.make_async_copy(fac_hbm.at[two(m)], fac_ref.at[two(m)], fac_sem.at[m]),
            pltpu.make_async_copy(z_hbm.at[two(m)], z_ref.at[two(m)], z_sem.at[m]),
        )

    def begin(m):
        for copy in came(m):
            copy.start()

    def step(m):
        for copy in came(m):
            copy.wait()
        made = jnp.concatenate([side_gradients(d_ref, fac_ref, m, h) for h in range(2)], axis=1)
        acc_ref[...] += dot(made, z_ref[two(m)].reshape(2 * total, C), 1, 0)

    each(rows // 2, begin)
    rest = pltpu.make_async_copy(sums_hbm, out_ref.at[pl.ds(4 * C, 2 * C)], sums_sem.at[0])
    rest.start()
    acc_ref[...] = jnp.zeros_like(acc_ref)
    each(rows // 2, step)
    for n in range(2):
        left, right = by_side(acc_ref[2 * C * n : 2 * C * (n + 1), :])
        out_ref[n * C : (n + 1) * C, :] = left.T
        out_ref[(2 + n) * C : (3 + n) * C, :] = right.T
    rest.wait()
    half = 3 * C
    keep = pl.multiple_of(lax.axis_index("core") * half, half)
    keep_ref[...] = out_ref[pl.ds(keep, half), :]
    give_ref[...] = out_ref[pl.ds(half - keep, half), :]


def pair_kernel(d_ref, fac_ref, dg_ref, w_ref, wg_ref, out_ref, wt_ref):
    rows = fac_ref.shape[0]
    wt_ref[...] = w_ref[...].astype(F32).T.astype(BF16)

    def body(m, carry):
        for h in range(2):
            i = 2 * m + h
            made = dot(wt_ref[...], side_gradients(d_ref, fac_ref, m, h), 1, 0)
            made += dot(wg_ref[...], dg_ref[m, h * C : (h + 1) * C, :], 1, 0)
            out_ref[0, i] = made.T.astype(BF16)
        return carry

    lax.fori_loop(0, rows // 2, body, 0)


def call(body, outs, scratch, flops, *args, smem=(), hbm=(), hbm_out=(), sems=(), after=(), limit=62):
    given = len(args)
    args = (*args, *after)
    hbm = (*hbm, *range(given, len(args)))

    def inner(*refs):
        body(*refs[:given], *refs[given + len(after) :])

    spaces = [pltpu.SMEM if n in smem else pltpu.HBM if n in hbm else pltpu.VMEM for n in range(len(args))]
    shapes = [jax.ShapeDtypeStruct(s, t) for s, t in outs]
    out_specs = [
        pl.BlockSpec(memory_space=pltpu.HBM if n in hbm_out else pltpu.VMEM) for n in range(len(outs))
    ]
    if len(outs) == 1:
        shapes, out_specs = shapes[0], out_specs[0]
    moved = sum(a.size * a.dtype.itemsize for a in args)
    return pl.pallas_call(
        inner,
        out_shape=shapes,
        in_specs=[pl.BlockSpec(memory_space=space) for space in spaces],
        out_specs=out_specs,
        scratch_shapes=[pltpu.VMEM(s, t) for s, t in scratch] + [pltpu.SemaphoreType.DMA((n,)) for n in sems],
        compiler_params=pltpu.CompilerParams(vmem_limit_bytes=limit << 20),
        cost_estimate=pl.CostEstimate(flops=flops, bytes_accessed=moved, transcendentals=0),
    )(*args)


def exchange(x, axis):
    return lax.all_to_all(x, axis, split_axis=0, concat_axis=0, tiled=True)


def swap(x):
    return lax.ppermute(x, "core", [(0, 1), (1, 0)])


def on_device(
    pair, cotangent, res_count, w_left, w_left_gate, w_right, w_right_gate, w_gate, w_out
):
    z, g = pair[0], cotangent[0]
    rows, total, _ = z.shape
    pairs = rows // 2
    sides = (w_left, w_left_gate, w_right, w_right_gate)
    mega = 10**6

    blocks = call(
        project_kernel, [((32, 8 * rows, total), BF16)],
        [((4 * C, C), BF16), ((rows, total, C), BF16), ((4, C, C), BF16), ((32, 8 * rows, total), BF16)],
        4000 * mega, res_count, z, *sides, smem=(0,), hbm=(1, 2, 3, 4, 5), hbm_out=(0,), sems=(pairs, 4, pairs),
    )
    factors, w_all = call(
        factors_kernel, [((rows, 4 * C, total), BF16), ((4 * C, C), BF16)], [], 4000 * mega,
        res_count, z, *sides, smem=(0,), after=(blocks,),
    )
    scaled, factor, spread, dnormed = call(
        gates_kernel,
        [((pairs, 2 * C, total), BF16), ((pairs, 2 * C, total), F32), ((2 * C, 2 * C), BF16),
         ((pairs, 2 * C, total), F32)],
        [((C, C), BF16)], 4000 * mega,
        z, g, w_gate, w_out, after=(blocks,),
    )
    blocks = exchange(blocks, DAP)
    edges = call(
        edges_kernel,
        [((32, 4 * rows, total), BF16)],
        [
            ((total // C, 8 * total, C), F32), ((total // C, 4 * total, C), F32),
            ((32, 8 * rows, total), BF16), ((32, 4 * rows, total), BF16),
        ], 4000 * mega,
        blocks, hbm=(0,), hbm_out=(0,), sems=(4, 4), after=(factors, scaled),
    )
    edges = exchange(edges, DAP)
    dedges = call(
        norm_kernel,
        [((32, 4 * rows, total), BF16)],
        [
            ((32, 4 * rows, total), BF16), ((pairs, 2 * C, total), F32), ((32, 4 * rows, total), BF16),
        ], 4000 * mega,
        res_count, edges, dnormed, smem=(0,), hbm=(1, 2), hbm_out=(0,), sems=(rows // 4,) * 3,
    )
    lr = call(
        split_kernel, [((8, total, total), BF16)],
        [((total // C, 8 * total, C), F32), ((32, 8 * rows, total), BF16)], 4000 * mega,
        blocks, hbm=(0,), sems=(4,), after=(dedges,),
    )
    dedges = exchange(dedges, DAP)
    back = call(
        back_kernel,
        [((32, 8 * rows, total), BF16)],
        [
            ((total // C, 4 * total, C), F32), ((total // C, 8 * total, C), F32),
            ((8, total, total), BF16), ((32, 4 * rows, total), BF16), ((32, 8 * rows, total), BF16),
        ], 4000 * mega,
        dedges, lr, hbm=(0, 1), hbm_out=(0,), sems=(4, 4, 4), limit=52,
    )
    dgate, sums = call(
        linear_kernel,
        [((pairs, 2 * C, total), BF16), ((2 * C, C), F32)],
        [((2 * C, 2 * C), BF16), ((pairs, 2 * C, total), BF16), ((C, C), F32), ((2 * C, 2 * C), F32)], 4000 * mega,
        res_count, z, edges, scaled, factor, spread, smem=(0,), after=(back,),
    )
    back = exchange(back, DAP)
    keep, give = call(
        weights_kernel,
        [((3 * C, C), F32), ((3 * C, C), F32)],
        [
            ((6 * C, C), F32), ((4 * C, C), F32), ((rows, total, C), BF16),
            ((32, 8 * rows, total), BF16), ((rows, 4 * C, total), BF16),
        ], 4000 * mega,
        z, back, factors, sums, hbm=(0, 1, 2, 3), sems=(pairs, pairs, pairs, 1), limit=52,
    )
    share = exchange((keep + swap(give)).reshape(16, 24, C), ("x", "y")).sum(axis=0, keepdims=True)
    share = exchange(jnp.broadcast_to(share, (8, 24, C)), "z").sum(axis=0, keepdims=True)
    share = jnp.broadcast_to(share, (16, 24, C))
    grad = call(
        pair_kernel,
        [((1, rows, total, C), BF16)],
        [((C, 4 * C), BF16)], 4000 * mega,
        back, factors, dgate, w_all, w_gate, after=(share,), limit=50,
    )
    mine, grad = lax.optimization_barrier((exchange(share, ("x", "y")), grad))
    mine = mine.reshape(3, C, C)
    other = swap(mine)
    first = lax.axis_index("core") == 0
    whole = [jnp.where(first, mine[n], other[n]) for n in range(3)]
    whole += [jnp.where(first, other[n], mine[n]) for n in range(3)]
    return (grad, *whole)


def solution(mesh):
    chips = Mesh(mesh.devices.reshape(4, 2, 8, 4), ISLAND + DAP)
    rows = P(ISLAND, DAP, None, None)
    return jax.shard_map(
        on_device,
        mesh=chips,
        in_specs=(rows, rows, P(ISLAND), P(), P(), P(), P(), P(), P()),
        out_specs=(rows, P(), P(), P(), P(), P(), P()),
        check_vma=False,
    )
```
